256 devices in a mesh: blk: 16 (over z_lo, y, core), uly: 16 (over x, z_hi).
Axes of the slice: x: 4, y: 4, z: 8 (z_hi: 4, z_lo: 2; z = z_hi * 2 + z_lo), core: 2. Of those that a mesh axis runs over, the one named last changes fastest.
Arguments:
- tokens: bfloat16 [16384, 4096], P(('blk', 'uly')), may hold values from -6 to 6
- norm_gain: float32 [4096], replicated, may hold values from 0.1 to 1.9
- w_qkv: bfloat16 [4096, 16, 384], P(None, 'uly')
- w_out: bfloat16 [16, 128, 4096], P('uly'), may hold values from -0.125 to 0.125
- positions: int32 [16384], replicated, may hold values from 0 to 16383, as said below
Outputs:
- attended: bfloat16 [16384, 4096], P(('blk', 'uly'))
The draws below stay inside these ranges and needn't reach their ends.
Inputs may be any that keep to these rules, and one draw needn't show every extreme that they name: positions is a permutation of 0 to 16383 made of 32 blocks of 512 consecutive positions; each block fills 512 aligned rows in ascending order; which block lies at which aligned rows is drawn from the seed.
All inputs are finite; a program needn't handle non-finite values.
Results may differ from the reference program's by a relative error of at most 0.02.
Values may be sent and summed in bfloat16 or wider, within the bound.
No kernel may reach another device: no remote copies, remote signals or barrier semaphores. Data moves between devices by JAX's collectives and lax.ppermute only.
A program may use at most 128 MiB of HBM per device.

```python
import math
import jax
import jax.numpy as jnp
from jax import lax

D = 4096
HEADS = 16
HD = 128
TOK_DEV = 64
HALF = 512
BLOCKS = 32
TOKENS = 16384
N_ULY = 16


def draw_positions(key, part):
    key = jax.random.fold_in(key, 5)
    order = jax.random.permutation(key, BLOCKS).astype(jnp.int32)
    inside = jnp.arange(HALF, dtype=jnp.int32)
    return (order[:, None] * HALF + inside[None, :]).reshape(-1).astype(jnp.int32)


def draw_w_qkv(key, part):
    key = jax.random.fold_in(key, 9)
    base = jax.random.normal(key, (D, HEADS, 3, HD), jnp.float32) * D ** (-0.5)
    packed = base
    return packed.reshape(D, HEADS, 3 * HD).astype(jnp.bfloat16)


def levels(stream_key, shape, shards, low, top_value):
    gain = 1.0
    for position, blocks in shards:
        draws = jax.random.uniform(jax.random.fold_in(jax.random.fold_in(stream_key, 6), position), (blocks,), jnp.float32, low / len(shards), top_value / len(shards))
        gain = gain * jnp.repeat(jnp.exp(draws), shape[position] // blocks).reshape((-1,) + (1,) * (len(shape) - 1 - position))
    return gain


def bell_draw(own_key, shape, width, bound, split=(), kind=jnp.bfloat16):
    array = width * jax.random.normal(own_key, shape, jnp.float32)
    if split:
        array = array * levels(own_key, shape, split, -0.22, 0.18)
    return jnp.clip(array, -bound, bound).astype(kind)


def setup_inputs(seed: int = 0) -> dict:
    splits = jax.random.split(jax.random.key(seed), 6)
    return {
        "tokens": bell_draw(splits[0], (TOKENS, D), 1.0, 6.0, ((0, 256),)),
        "norm_gain": jnp.clip(1.0 + 0.18 * jax.random.normal(splits[1], (D,), jnp.float32), 0.1, 1.9),
        "w_qkv": draw_w_qkv(jax.random.fold_in(splits[5], 71), 0),
        "w_out": bell_draw(splits[3], (HEADS, HD, D), (HEADS * HD) ** -0.5, 0.125, ((0, 16),)),
        "positions": draw_positions(jax.random.fold_in(splits[5], 71), 0),
    }


def rope_tables(places, head_size):
    freqs = jnp.exp(jnp.arange(head_size // 2, dtype=jnp.float32) * (-2.0 * math.log(10000.0) / head_size))
    angles = places.astype(jnp.float32)[:, None] * freqs[None, :]
    return (jnp.cos(angles)[:, None, :], jnp.sin(angles)[:, None, :])

def rotate(values, cosines, sines):
    half_width = values.shape[-1] // 2
    first = values[..., :half_width]
    second = values[..., half_width:]
    return jnp.concatenate([first * cosines - second * sines, second * cosines + first * sines], axis=-1)

def project(normed, w_qkv, places):
    packed = jnp.einsum('td,dhe->the', normed.astype(jnp.float32), w_qkv.astype(jnp.float32))
    head_size = w_qkv.shape[2] // 3
    cosines, sines = rope_tables(places, head_size)
    query = rotate(packed[..., :head_size], cosines, sines) / math.sqrt(head_size)
    key = rotate(packed[..., head_size:2 * head_size], cosines, sines)
    value = packed[..., 2 * head_size:]
    return (query.astype(jnp.bfloat16), key.astype(jnp.bfloat16), value.astype(jnp.bfloat16))

def reference(tokens, norm_gain, w_qkv, w_out, positions):
    values = tokens.astype(jnp.float32)
    normed = (values * lax.rsqrt(lax.optimization_barrier(jnp.mean(values * values, axis=-1, keepdims=True)) + 1e-05) * norm_gain).astype(jnp.bfloat16)
    query, key, value = project(normed, w_qkv, positions)
    query = jnp.transpose(query, (1, 0, 2))
    key = jnp.transpose(key, (1, 0, 2))
    value = jnp.transpose(value, (1, 0, 2))
    group = TOK_DEV * N_ULY
    count = TOKENS // group

    def one_head(operands):
        head_query, head_key, head_value = operands

        def one_block(index):
            start = (index * group).astype(jnp.int32)
            rows = lax.dynamic_slice_in_dim(head_query, start, group, 0)
            row_places = lax.dynamic_slice_in_dim(positions, start, group, 0)
            scores = jnp.dot(rows, head_key.T, preferred_element_type=jnp.float32)
            keep = positions[None, :] <= row_places[:, None]
            scores = jnp.where(keep, scores, -jnp.inf)
            top = lax.optimization_barrier(jnp.max(scores, axis=-1, keepdims=True))
            weights = jnp.exp(scores - top)
            total = lax.optimization_barrier(jnp.sum(weights, axis=-1, keepdims=True))
            mixed = jnp.dot(weights.astype(jnp.bfloat16), head_value, preferred_element_type=jnp.float32)
            return (mixed / total).astype(jnp.bfloat16)
        blocks = lax.map(one_block, jnp.arange(count, dtype=jnp.int32))
        return blocks.reshape(TOKENS, head_query.shape[-1])
    context = lax.map(one_head, (query, key, value))
    context = jnp.transpose(context, (1, 0, 2)).reshape(TOKENS, HEADS * HD)
    attended = jnp.dot(context, w_out.reshape(HEADS * HD, D), preferred_element_type=jnp.float32)
    return attended.astype(jnp.bfloat16)
```

```python
import functools
import math

import jax
import jax.numpy as jnp
from jax import lax
from jax.experimental import pallas as pl
from jax.experimental.pallas import tpu as pltpu
from jax.sharding import PartitionSpec as P

HALF = 512
HD = 128
LOW = -1e30
EXTRA = 144
N_Y = 4
BF16 = jnp.bfloat16
F32 = jnp.float32


def blk_route(move):
    route = []
    for z in range(2):
        for y in range(N_Y):
            for c in range(2):
                a, b, e = move(z, y, c)
                route.append((z * 8 + y * 2 + c, (a % 2) * 8 + (b % N_Y) * 2 + e % 2))
    return route


def along_y(array, distance):
    return lax.ppermute(array, "blk", blk_route(lambda z, y, c: (z, y + distance, c)))


def to_partner(array, dz, dc):
    return lax.ppermute(array, "blk", blk_route(lambda z, y, c: (z + dz, y, c + dc)))


def rope_tables(places):
    freqs = jnp.exp(jnp.arange(HD // 2, dtype=F32) * (-2.0 * math.log(10000.0) / HD))
    angles = places.astype(F32)[:, None] * freqs[None, :]
    cos, sin = jnp.cos(angles), jnp.sin(angles)
    return jnp.concatenate([cos, cos], 1), jnp.concatenate([-sin, sin], 1)


def project_body(x_ref, w_ref, cos_ref, sin_ref, qt_ref, k_ref, vt_ref):
    packed = jnp.dot(x_ref[...], w_ref[...], preferred_element_type=F32)

    def rot(part):
        return part * cos_ref[...] + pltpu.roll(part, HD // 2, 1) * sin_ref[...]

    query = rot(packed[:, :HD]) * (math.log2(math.e) / math.sqrt(HD))
    qt_ref[...] = query.T.astype(BF16)
    k_ref[...] = rot(packed[:, HD : 2 * HD]).astype(BF16)
    vt_ref[...] = packed[:, 2 * HD :].T.astype(BF16)


def project(x, w, cos, sin):
    rows, width = x.shape
    tile = 256
    return pl.pallas_call(
        project_body,
        grid=(rows // tile,),
        in_specs=[
            pl.BlockSpec((tile, width), lambda i: (i, 0)),
            pl.BlockSpec(w.shape, lambda i: (0, 0)),
            pl.BlockSpec((tile, HD), lambda i: (i, 0)),
            pl.BlockSpec((tile, HD), lambda i: (i, 0)),
        ],
        out_specs=[
            pl.BlockSpec((HD, tile), lambda i: (0, i)),
            pl.BlockSpec((tile, HD), lambda i: (i, 0)),
            pl.BlockSpec((HD, tile), lambda i: (0, i)),
        ],
        out_shape=[
            jax.ShapeDtypeStruct((HD, rows), BF16),
            jax.ShapeDtypeStruct((rows, HD), BF16),
            jax.ShapeDtypeStruct((HD, rows), BF16),
        ],
        compiler_params=pltpu.CompilerParams(vmem_limit_bytes=40 << 20),
        cost_estimate=pl.CostEstimate(
            flops=2 * rows * width * 3 * HD, bytes_accessed=12 << 20, transcendentals=0
        ),
    )(x, w, cos, sin)


def attend_body(first, last, n_keys, order, q_block, k_block, *refs):
    n_q = 8
    refs = list(refs)
    if first:
        q_parts = [refs.pop(0) for _ in range(4)]
    else:
        q_in, acc_in, top_in = refs.pop(0), refs.pop(0), refs.pop(0)
    k_refs = [refs.pop(0) for _ in range(n_keys // 2)]
    v_refs = [refs.pop(0) for _ in range(n_keys // 2)]
    if last:
        out_ref, lse_ref = refs.pop(0), refs.pop(0)
        if first:
            q_sorted, acc, top = refs
        else:
            q_sorted = q_in
            acc, top = refs
    else:
        if first:
            q_sorted, acc, top = refs
        else:
            q_sorted = q_in
            acc, top = refs
    if first:
        for rank in range(n_q):
            for part in range(4):
                for half in range(2):

                    @pl.when(order[rank] == 2 * part + half)
                    def _(rank=rank, part=part, half=half):
                        q_sorted[:, rank * HALF : (rank + 1) * HALF] = q_parts[part][
                            :, half * HALF : (half + 1) * HALF
                        ]

        acc[...] = jnp.zeros_like(acc)
        top[...] = jnp.full_like(top, LOW)
    else:
        acc[...] = acc_in[...]
        top[...] = top_in[...]

    def tile(k_ref, v_ref, start, offset, width, on_diagonal):
        cols = pl.ds(pl.multiple_of(offset, HALF), width)
        keys = k_ref[start : start + HALF, :]
        values = jnp.concatenate(
            [v_ref[:, start : start + HALF], jnp.ones((EXTRA - HD, HALF), BF16)], axis=0
        )
        scores = jnp.dot(keys, q_sorted[:, cols], preferred_element_type=F32)
        key_at = lax.broadcasted_iota(jnp.int32, (HALF, HALF), 0)
        query_at = lax.broadcasted_iota(jnp.int32, (HALF, HALF), 1)
        reach = jnp.where(on_diagonal, 0, HALF)
        head = jnp.where(key_at <= query_at + reach, scores[:, :HALF], LOW)
        scores = head if width == HALF else jnp.concatenate([head, scores[:, HALF:]], axis=1)
        old = top[:1, cols]
        new = jnp.maximum(old, jnp.max(scores, axis=0, keepdims=True))
        weights = jnp.exp2(scores - new).astype(BF16)
        acc[:, cols] = acc[:, cols] * jnp.exp2(old - new) + jnp.dot(
            values, weights, preferred_element_type=F32
        )
        top[:, cols] = jnp.broadcast_to(new, (8, width))

    for j in range(n_keys):
        k_ref, v_ref, start = k_refs[j // 2], v_refs[j // 2], (j % 2) * HALF
        block = k_block[j]
        count = jnp.int32(0)
        diagonal = jnp.int32(0)
        for i in range(n_q):
            count += (q_block[i] >= block).astype(jnp.int32)
            diagonal += (q_block[i] == block).astype(jnp.int32)
        is_diagonal = diagonal > 0
        has1, has2, has4, has8 = (count & 1) > 0, (count & 2) > 0, (count & 4) > 0, count >= 8
        begin = (n_q - count) * HALF

        @pl.when(has1)
        def _():
            tile(k_ref, v_ref, start, begin, HALF, is_diagonal)

        at2 = begin + (count & 1) * HALF

        @pl.when(has2)
        def _():
            tile(k_ref, v_ref, start, at2, 2 * HALF, is_diagonal & jnp.logical_not(has1))

        @pl.when(has4 | has8)
        def _():
            first_in = jnp.logical_not(has1 | has2)
            at4 = jnp.where(has8, 0, 4 * HALF)
            tile(k_ref, v_ref, start, at4, 4 * HALF, is_diagonal & first_in)

        @pl.when(has8)
        def _():
            tile(k_ref, v_ref, start, 4 * HALF, 4 * HALF, False)

    if last:
        total = acc[HD : HD + 1, :]
        seen = total > 0
        safe = jnp.where(seen, total, 1.0)
        lse = jnp.where(seen, top[:1, :] + jnp.log2(safe), LOW)
        for rank in range(n_q):
            cols = slice(rank * HALF, (rank + 1) * HALF)
            at = pl.ds(pl.multiple_of(order[rank] * HALF, HALF), HALF)
            out_ref[:, at] = (acc[:HD, cols] / safe[:, cols]).astype(BF16)
            lse_ref[:, at] = jnp.broadcast_to(lse[:, cols], (8, HALF))


def attend(order, q_block, k_block, q_parts, state, keys, values, last):
    first = state is None
    n_keys = 2 * len(keys)
    q_cols = 4096
    smem = pl.BlockSpec(memory_space=pltpu.SMEM)
    vmem = pl.BlockSpec(memory_space=pltpu.VMEM)
    state_shapes = [
        jax.ShapeDtypeStruct((HD, q_cols), BF16),
        jax.ShapeDtypeStruct((EXTRA, q_cols), F32),
        jax.ShapeDtypeStruct((8, q_cols), F32),
    ]
    state_scratch = [
        pltpu.VMEM((HD, q_cols), BF16),
        pltpu.VMEM((EXTRA, q_cols), F32),
        pltpu.VMEM((8, q_cols), F32),
    ]
    args = list(q_parts) if first else list(state)
    if last:
        out_shape = [
            jax.ShapeDtypeStruct((HD, q_cols), BF16),
            jax.ShapeDtypeStruct((8, q_cols), F32),
        ]
        scratch = state_scratch if first else state_scratch[1:]
    else:
        out_shape = state_shapes if first else state_shapes[1:]
        scratch = []
    args += list(keys) + list(values)
    pairs = n_keys * 5
    outs = pl.pallas_call(
        functools.partial(attend_body, first, last, n_keys),
        in_specs=[smem] * 3 + [vmem] * len(args),
        out_specs=[vmem] * len(out_shape),
        out_shape=out_shape,
        scratch_shapes=scratch,
        compiler_params=pltpu.CompilerParams(vmem_limit_bytes=56 << 20),
        cost_estimate=pl.CostEstimate(
            flops=pairs * HALF * HALF * HD * 4,
            bytes_accessed=8 << 20,
            transcendentals=pairs * HALF * HALF,
        ),
    )(order, q_block, k_block, *args)
    if last:
        return outs
    return outs if first else [state[0]] + list(outs)


def merge_body(*refs):
    outs, lses, context_ref = refs[:4], refs[4:8], refs[8]
    top = functools.reduce(jnp.maximum, [lse[:1, :] for lse in lses])
    shares = [jnp.exp2(lse[:1, :] - top) for lse in lses]
    total = functools.reduce(jnp.add, shares)
    mixed = functools.reduce(
        jnp.add, [out[...].astype(F32) * share for out, share in zip(outs, shares)]
    )
    context_ref[...] = (mixed / total).T.astype(BF16)


def merge(outs, lses):
    rows = outs[0].shape[1]
    vmem = pl.BlockSpec(memory_space=pltpu.VMEM)
    return pl.pallas_call(
        merge_body,
        in_specs=[vmem] * 8,
        out_specs=vmem,
        out_shape=jax.ShapeDtypeStruct((rows, HD), BF16),
    )(*outs, *lses)


def output_body(x0, x1, x2, x3, w_ref, o0, o1, o2, o3):
    rows = jnp.concatenate(
        [
            jnp.concatenate([x[h] for h in range(x.shape[0])], axis=1)
            for x in (x0, x1, x2, x3)
        ],
        axis=0,
    )
    out = jnp.dot(rows, w_ref[...], preferred_element_type=F32).astype(BF16)
    n = x0.shape[1]
    for i, o in enumerate((o0, o1, o2, o3)):
        o[...] = out[i * n : (i + 1) * n]


def output(parts, w):
    n = parts[0].shape[1]
    tile = 256
    return pl.pallas_call(
        output_body,
        grid=(w.shape[1] // tile,),
        in_specs=[pl.BlockSpec(parts[0].shape, lambda i: (0, 0, 0))] * 4
        + [pl.BlockSpec((w.shape[0], tile), lambda i: (0, i))],
        out_specs=[pl.BlockSpec((n, tile), lambda i: (0, i))] * 4,
        out_shape=[jax.ShapeDtypeStruct((n, w.shape[1]), BF16)] * 4,
        compiler_params=pltpu.CompilerParams(vmem_limit_bytes=32 << 20),
    )(*parts, w)


def place_body(y_ref, x0, x1, x2, x3, out_ref):
    width = x0.shape[1]
    for d, x in enumerate((x0, x1, x2, x3)):
        quarter = lax.rem(y_ref[0] - d + N_Y, N_Y)
        out_ref[:, pl.ds(pl.multiple_of(quarter * width, width), width)] = x[...]


def place(y, parts):
    rows, width = parts[0].shape
    vmem = pl.BlockSpec(memory_space=pltpu.VMEM)
    return pl.pallas_call(
        place_body,
        in_specs=[pl.BlockSpec(memory_space=pltpu.SMEM)] + [vmem] * 4,
        out_specs=vmem,
        out_shape=jax.ShapeDtypeStruct((rows, 4 * width), BF16),
    )(y.reshape(1), *parts)


def shards(tokens, norm_gain, w_qkv, w_out, positions):
    tok_dev, width = tokens.shape
    n_uly = lax.axis_size("uly")
    group = tok_dev * n_uly
    blk = lax.axis_index("blk")
    z, y, c = blk // 8, (blk // 2) % N_Y, blk % 2

    values_in = tokens.astype(F32)
    normed = (
        values_in
        * lax.rsqrt(jnp.mean(values_in * values_in, axis=-1, keepdims=True) + 1e-05)
        * norm_gain
    ).astype(BF16)
    piece = lax.all_gather(normed, "uly", axis=0, tiled=True)
    quarter = w_out.shape[2] // N_Y
    w_mine = lax.dynamic_slice_in_dim(w_out[0], y * quarter, quarter, 1)
    w_cols = lax.all_gather(w_mine, "uly", axis=0, tiled=True)

    places = lax.dynamic_slice_in_dim(positions, blk * group, group, 0)
    cos, sin = rope_tables(places)
    qt, k, vt = project(piece, w_qkv[:, 0, :], cos, sin)

    block_of = positions[::HALF] // HALF
    moves = [(0, 0), (0, 1), (1, 0), (1, 1)]
    q_groups = jnp.stack([((z + dz) % 2) * 8 + y * 2 + (c + dc) % 2 for dz, dc in moves])
    q_ids = block_of[(q_groups[:, None] * 2 + jnp.arange(2)[None, :]).reshape(-1)]
    ranks = jnp.sum(q_ids[None, :] < q_ids[:, None], axis=1)
    at_rank = ranks[None, :] == jnp.arange(8)[:, None]
    order = jnp.sum(jnp.where(at_rank, jnp.arange(8)[None, :], 0), axis=1).astype(jnp.int32)
    q_block = jnp.sum(jnp.where(at_rank, q_ids[None, :], 0), axis=1).astype(jnp.int32)

    def key_ids(distances):
        groups = jnp.stack([z * 8 + ((y - d) % N_Y) * 2 + c for d in distances])
        return block_of[(groups[:, None] * 2 + jnp.arange(2)[None, :]).reshape(-1)]

    q_parts = [qt] + [to_partner(qt, dz, dc) for dz, dc in moves[1:]]
    near = [1, 3]
    k_near = [along_y(k, d) for d in near]
    v_near = [along_y(vt, d) for d in near]
    k_far, v_far = along_y(k, 2), along_y(vt, 2)
    state = attend(order, q_block, key_ids([0]), q_parts, None, [k], [vt], False)
    state = attend(order, q_block, key_ids(near), None, state, k_near, v_near, False)
    out, lse = attend(order, q_block, key_ids([2]), None, state, [k_far], [v_far], True)

    def mine(array, i):
        return array[:, i * group : (i + 1) * group]

    outs, lses = [mine(out, 0)], [mine(lse, 0)]
    for i, (dz, dc) in enumerate(moves[1:], 1):
        outs.append(to_partner(mine(out, i), dz, dc))
        lses.append(to_partner(mine(lse, i), dz, dc))
    context = merge(outs, lses)

    heads = lax.all_to_all(context.reshape(n_uly, tok_dev, HD), "uly", 0, 0)
    rows = [heads] + [along_y(heads, -d) for d in (1, 2, 3)]
    made = output(rows, w_cols)
    parts = [made[0]] + [along_y(made[d], d) for d in (1, 2, 3)]
    return place(y, parts)


def solution(mesh):
    placed = (P(("blk", "uly"), None), P(), P(None, "uly", None), P("uly", None, None), P())
    return jax.shard_map(
        shards, mesh=mesh, in_specs=placed, out_specs=P(("blk", "uly"), None), check_vma=False
    )
```

```python
import functools
import math

import jax
import jax.numpy as jnp
from jax import lax
from jax.experimental import pallas as pl
from jax.experimental.pallas import tpu as pltpu
from jax.sharding import PartitionSpec as P

HALF = 512
HD = 128
LOW = -1e30
EXTRA = 144
N_X, N_Y, N_Z = 4, 4, 4
TOK = 64
SUB = 2 * TOK
BF16 = jnp.bfloat16
F32 = jnp.float32
SMEM = pl.BlockSpec(memory_space=pltpu.SMEM)
VMEM = pl.BlockSpec(memory_space=pltpu.VMEM)
ANY = pl.BlockSpec(memory_space=pl.ANY)
BOTH = ("blk", "uly")


def route(move):
    pairs = []
    for x in range(N_X):
        for y in range(N_Y):
            for z in range(2 * N_Z):
                for c in range(2):
                    a, b, d, e = move(x, y, z, c)
                    pairs.append((number(x, y, z, c), number(a % N_X, b % N_Y, d, e)))
    return pairs


def number(x, y, z, c):
    return ((z % 2) * 8 + y * 2 + c) * 16 + x * N_Z + z // 2


def along_x(array, distance):
    return lax.ppermute(array, BOTH, route(lambda x, y, z, c: (x + distance, y, z, c)))


def along_y(array, distance):
    return lax.ppermute(array, BOTH, route(lambda x, y, z, c: (x, y + distance, z, c)))


def to_mirror(array):
    return lax.ppermute(array, BOTH, route(lambda x, y, z, c: (x, y, 7 - z, c)))


def to_swap(array):
    return lax.ppermute(array, BOTH, route(lambda x, y, z, c: (x, y, z ^ 2, c)))


def to_twin(array):
    return lax.ppermute(array, BOTH, route(lambda x, y, z, c: (x, y, z ^ 1, c)))


def to_other_core(array):
    return lax.ppermute(array, BOTH, route(lambda x, y, z, c: (x, y, z, 1 - c)))


def after(values, done):
    return lax.optimization_barrier((values, done))[0]


def rope_tables(places):
    freqs = jnp.exp(jnp.arange(HD // 2, dtype=F32) * (-2.0 * math.log(10000.0) / HD))
    angles = places.astype(F32)[:, None] * freqs[None, :]
    cos, sin = jnp.cos(angles), jnp.sin(angles)
    return jnp.concatenate([cos, cos], 1), jnp.concatenate([-sin, sin], 1)


def norm_body(x_ref, gain_ref, out_ref):
    x = x_ref[...].astype(F32)
    scale = lax.rsqrt(jnp.mean(x * x, axis=-1, keepdims=True) + 1e-05)
    out_ref[...] = (x * scale * gain_ref[...]).astype(BF16)


def norm(tokens, gain):
    rows, width = tokens.shape
    return pl.pallas_call(
        norm_body,
        in_specs=[VMEM, VMEM],
        out_specs=VMEM,
        out_shape=jax.ShapeDtypeStruct((rows, width), BF16),
    )(tokens, gain.reshape(1, width))


def start_copies(pairs, sems):
    copies = [pltpu.make_async_copy(a, b, sems.at[i]) for i, (a, b) in enumerate(pairs)]
    for copy in copies:
        copy.start()
    return copies


def row_places(refs, buffer):
    pairs, at = [], 0
    for ref in refs:
        pairs.append((ref, buffer.at[at : at + ref.shape[0]]))
        at += ref.shape[0]
    return pairs


def partial_body(*refs):
    x_refs, w_ref, out_ref, rows, w, sems = refs[:-5], *refs[-5:]
    for copy in start_copies(row_places(x_refs, rows) + [(w_ref, w)], sems):
        copy.wait()
    out_ref[...] = jnp.dot(rows[...], w[...], preferred_element_type=F32)


def partial_product(arrays, w):
    rows = sum(a.shape[0] for a in arrays)
    return pl.pallas_call(
        partial_body,
        in_specs=[ANY] * (len(arrays) + 1),
        out_specs=VMEM,
        out_shape=jax.ShapeDtypeStruct((rows, w.shape[1]), F32),
        scratch_shapes=[
            pltpu.VMEM((rows, w.shape[0]), BF16),
            pltpu.VMEM(w.shape, BF16),
            pltpu.SemaphoreType.DMA((len(arrays) + 1,)),
        ],
        compiler_params=pltpu.CompilerParams(vmem_limit_bytes=60 << 20),
        cost_estimate=pl.CostEstimate(
            flops=2 * rows * w.shape[0] * w.shape[1], bytes_accessed=6 << 20, transcendentals=0
        ),
    )(*arrays, w)


def project_body(n_far, at_ref, *refs):
    far_refs, refs = refs[:n_far], refs[n_far:]
    hbm, (q_ref, kv_ref, other_ref), (rows, packed) = refs[:6], refs[6:9], refs[9:11]
    buffers, sems = refs[11:-1], refs[-1]
    w_refs, own_refs, (cos_ref, sin_ref) = buffers[:2], buffers[2:4], buffers[4:]
    copies = start_copies(row_places(far_refs, rows) + list(zip(hbm, buffers)), sems)
    x, e_own = at_ref[0], at_ref[1]
    for copy in copies[:n_far]:
        copy.wait()
    copies = copies[n_far:]
    span = N_X * TOK
    for h in range(2):
        copies[h].wait()
        far = jnp.dot(rows[...], w_refs[h][...], preferred_element_type=F32)
        copies[2 + h].wait()
        for j, dx in enumerate((0, 1, -1, 2)):
            source = lax.rem(x + dx + N_X, N_X) * TOK
            piece = slice(j * TOK, (j + 1) * TOK)
            own_at = pl.ds(pl.multiple_of(e_own * span + source, TOK), TOK)
            far_at = pl.ds(pl.multiple_of((1 - e_own) * span + source, TOK), TOK)
            packed[own_at, :] = own_refs[h][piece, :]
            packed[far_at, :] = far[piece, :]
        if h == 0:
            copies[4].wait()
            copies[5].wait()
        for s in range(4):
            at = slice(s * SUB, (s + 1) * SUB)
            cos, sin = cos_ref[at, :], sin_ref[at, :]

            def rot(part):
                return part * cos + pltpu.roll(part, HD // 2, 1) * sin

            query = rot(packed[at, :HD]) * (math.log2(math.e) / math.sqrt(HD))
            query = query.T.astype(BF16)
            key = rot(packed[at, HD : 2 * HD]).astype(BF16)
            value = packed[at, 2 * HD :].T.astype(BF16)
            if h == 0:
                q_ref[s] = query
                kv_ref[s, :SUB] = key
                kv_ref[s, SUB:] = value
            else:
                other_ref[s, :HD] = query
                other_ref[s, HD : HD + SUB] = key
                other_ref[s, HD + SUB :] = value


def project(at, far, ws, owns, cos, sin):
    arrays = [*ws, *owns, cos, sin]
    n_copies = len(far) + len(arrays)
    rows = cos.shape[0]
    return pl.pallas_call(
        functools.partial(project_body, len(far)),
        in_specs=[SMEM] + [ANY] * n_copies,
        out_specs=[VMEM] * 3,
        out_shape=[
            jax.ShapeDtypeStruct((4, HD, SUB), BF16),
            jax.ShapeDtypeStruct((4, 2 * SUB, HD), BF16),
            jax.ShapeDtypeStruct((4, 3 * SUB, HD), BF16),
        ],
        scratch_shapes=[
            pltpu.VMEM((rows // 2, far[0].shape[1]), BF16),
            pltpu.VMEM((rows, 3 * HD), F32),
        ]
        + [pltpu.VMEM(a.shape, a.dtype) for a in arrays]
        + [pltpu.SemaphoreType.DMA((n_copies,))],
        compiler_params=pltpu.CompilerParams(vmem_limit_bytes=60 << 20),
        cost_estimate=pl.CostEstimate(
            flops=rows * 4096 * 6 * HD, bytes_accessed=9 << 20, transcendentals=0
        ),
    )(at, *far, *arrays)


def attend_body(first, last, steps, block_of, at_ref, *refs):
    n_q = 8
    width_q = 2 * SUB
    refs = list(refs)
    take = lambda n: [refs.pop(0) for _ in range(n)]
    n_arrays = sum(len(views) for _, views in steps)
    if first:
        q_parts = take(2)
    else:
        q_sorted, acc_in, top_in = take(3)
    kv_in = take(n_arrays)
    if last:
        outs = take(2)
        acc, top = take(2)
    elif first:
        q_sorted, acc, top = take(3)
    else:
        acc, top = take(2)
    kv_refs = take(n_arrays)
    (sems,) = take(1)
    copies = start_copies(list(zip(kv_in, kv_refs)), sems)

    y, c, k = at_ref[2], at_ref[3], at_ref[4]

    def id_of(e, dy, core, x_hi):
        return block_of[(e * 8 + lax.rem(y + dy + N_Y, N_Y) * 2 + core) * 2 + x_hi]

    q_ids = [id_of(s // 2, 0, core, s % 2) for core in (c, 1 - c) for s in range(4)]
    ranks = [
        functools.reduce(
            jnp.add, [(q_ids[u] < q_ids[v]).astype(jnp.int32) for u in range(n_q) if u != v]
        )
        for v in range(n_q)
    ]
    spots = [pl.ds(pl.multiple_of(rank * width_q, width_q), width_q) for rank in ranks]
    if first:
        for v in range(n_q):
            part, s = q_parts[v // 4], v % 4
            q_sorted[:, spots[v]] = jnp.concatenate([part[s], part[4 + s]], axis=1)
        acc[...] = jnp.zeros_like(acc)
        top[...] = jnp.full_like(top, LOW)
    else:
        acc[...] = acc_in[...]
        top[...] = top_in[...]

    def place_of(index, ks, e):
        run, inside = index // SUB, index % SUB
        at = (inside // TOK) * (N_Z * TOK) + inside % TOK
        for i, kk in enumerate(ks):
            zh = jnp.where(e == 0, kk, 3 - kk)
            at = at + jnp.where(run == i, zh * TOK, 0)
        return at

    other = 3 - k
    key_ks = [k, k ^ 1, other, other ^ 1]

    def tile(load, offset, width, masks):
        cols = pl.ds(pl.multiple_of(offset, HALF), width)
        keys, values, e, near, far = load()
        scores = jnp.dot(keys, q_sorted[:, cols], preferred_element_type=F32)
        key_at = place_of(lax.broadcasted_iota(jnp.int32, (HALF, 1), 0), key_ks, e)
        query = lax.broadcasted_iota(jnp.int32, (1, HALF), 1)
        query_at = place_of(query % width_q, key_ks[:2], e)
        reach = jnp.where(masks, jnp.where(query < width_q, near, far), 2 * HALF)
        head = jnp.where(key_at <= query_at + reach, scores[:, :HALF], LOW)
        scores = head if width == HALF else jnp.concatenate([head, scores[:, HALF:]], axis=1)
        old = top[:1, cols]
        new = jnp.maximum(old, jnp.max(scores, axis=0, keepdims=True))
        weights = jnp.exp2(scores - new).astype(BF16)
        acc[:, cols] = acc[:, cols] * jnp.exp2(old - new) + jnp.dot(
            values, weights, preferred_element_type=F32
        )
        top[:, cols] = jnp.broadcast_to(new, (8, width))

    def key_block(dy, views, s):
        e = s // 2
        block = id_of(e, dy, c, lax.rem(s, 2))
        count = functools.reduce(jnp.add, [(i >= block).astype(jnp.int32) for i in q_ids])
        same = functools.reduce(jnp.add, [(i == block).astype(jnp.int32) for i in q_ids]) > 0
        odd = lax.rem(count, 2) > 0
        edge = jnp.where(same, 0, 2 * HALF)
        near = jnp.where(odd, -2 * HALF, edge)
        far = jnp.where(odd, edge, 2 * HALF)
        pairs = (count + 1) // 2
        begin = (n_q // 2 - pairs) * HALF

        def load():
            runs = [ref[base + s] for ref, base in views]
            keys = jnp.concatenate([r[:SUB] for r in runs], axis=0)
            values = jnp.concatenate([r[SUB:] for r in runs], axis=1)
            values = jnp.concatenate([values, jnp.ones((EXTRA - HD, HALF), BF16)], axis=0)
            return keys, values, e, near, far

        has1 = (pairs & 1) > 0

        @pl.when(has1)
        def _():
            tile(load, begin, HALF, True)

        @pl.when((pairs & 2) > 0)
        def _():
            tile(load, begin + (pairs & 1) * HALF, 2 * HALF, jnp.logical_not(has1))

        @pl.when(pairs >= 4)
        def _():
            tile(load, 0, 4 * HALF, True)

    used = 0
    for dy, bases in steps:
        n = len(bases)
        for copy in copies[used : used + n]:
            copy.wait()
        views = [
            (ref, base) for ref, which in zip(kv_refs[used : used + n], bases) for base in which
        ]
        used += n

        @pl.loop(0, 4)
        def _(s, dy=dy, views=views):
            key_block(dy, views, s)

    if last:
        for v in range(n_q):
            total = acc[HD : HD + 1, spots[v]]
            seen = total > 0
            safe = jnp.where(seen, total, 1.0)
            lse = jnp.where(seen, top[:1, spots[v]] + jnp.log2(safe), LOW)
            high = lse.astype(BF16).astype(F32)
            middle = (lse - high).astype(BF16).astype(F32)
            low = lse - high - middle
            row = lax.broadcasted_iota(jnp.int32, (EXTRA - HD, width_q), 0)
            tail = jnp.where(row == 0, high, jnp.where(row == 1, middle, jnp.where(row == 2, low, 0)))
            cols = slice((v % 4) * width_q, (v % 4 + 1) * width_q)
            outs[v // 4][:HD, cols] = (acc[:HD, spots[v]] / safe).astype(BF16)
            outs[v // 4][HD:, cols] = tail.astype(BF16)


def attend(block_of, at, q_parts, state, steps, arrays, last):
    first = state is None
    q_cols = 4 * HALF
    q_shape, acc_shape, top_shape = (HD, q_cols), (EXTRA, q_cols), (8, q_cols)
    args = list(q_parts if first else state) + list(arrays)
    if last:
        out_shape = [jax.ShapeDtypeStruct((EXTRA, q_cols // 2), BF16)] * 2
        scratch = [pltpu.VMEM(acc_shape, F32), pltpu.VMEM(top_shape, F32)]
    else:
        out_shape = [jax.ShapeDtypeStruct(q_shape, BF16)] if first else []
        out_shape += [
            jax.ShapeDtypeStruct(acc_shape, F32),
            jax.ShapeDtypeStruct(top_shape, F32),
        ]
        scratch = []
    scratch += [pltpu.VMEM(a.shape, a.dtype) for a in arrays]
    scratch.append(pltpu.SemaphoreType.DMA((len(arrays),)))
    pairs = 8 * len(steps)
    outs = pl.pallas_call(
        functools.partial(attend_body, first, last, steps),
        in_specs=[SMEM] * 2 + [VMEM] * (len(args) - len(arrays)) + [ANY] * len(arrays),
        out_specs=[VMEM] * len(out_shape),
        out_shape=out_shape,
        scratch_shapes=scratch,
        compiler_params=pltpu.CompilerParams(vmem_limit_bytes=48 << 20),
        cost_estimate=pl.CostEstimate(
            flops=pairs * HALF * HALF * HD * 4,
            bytes_accessed=6 << 20,
            transcendentals=pairs * HALF * HALF,
        ),
    )(block_of, at, *args)
    if last or first:
        return outs
    return [state[0]] + list(outs)


def merge_body(at_ref, own_ref, other_ref, context_ref):
    parts = [own_ref, other_ref]
    lses = []
    for ref in parts:
        tail = ref[HD:, :].astype(F32)
        lses.append(tail[0:1, :] + tail[1:2, :] + tail[2:3, :])
    top = jnp.maximum(*lses)
    shares = [jnp.exp2(lse - top) for lse in lses]
    mixed = [ref[:HD, :].astype(F32) * share for ref, share in zip(parts, shares)]
    context = ((mixed[0] + mixed[1]) / (shares[0] + shares[1])).T.astype(BF16)
    k = at_ref[4]
    for s in range(4):
        for i in range(2):
            kk = k if i == 0 else k ^ 1
            zh = kk if s < 2 else 3 - kk
            for x_lo in range(2):
                x = (s % 2) * 2 + x_lo
                start = (s * 2 + i) * SUB + x_lo * TOK
                at = pl.ds(pl.multiple_of((x * N_Z + zh) * TOK, TOK), TOK)
                context_ref[at, :] = context[start : start + TOK, :]


def merge(at, own, other):
    return pl.pallas_call(
        merge_body,
        in_specs=[SMEM] + [VMEM] * 2,
        out_specs=VMEM,
        out_shape=jax.ShapeDtypeStruct((own.shape[1], HD), BF16),
    )(at, own, other)


def output_body(x0, x1, x2, x3, w0, w1, o0, o1, o2, o3):
    rows = jnp.concatenate(
        [
            jnp.concatenate([x[h] for h in range(x.shape[0])], axis=1)
            for x in (x0, x1, x2, x3)
        ],
        axis=0,
    )
    w = jnp.where(pl.program_id(0) < 2, w0[...], w1[...])
    out = jnp.dot(rows, w, preferred_element_type=F32).astype(BF16)
    n = x0.shape[1]
    for i, o in enumerate((o0, o1, o2, o3)):
        o[...] = out[i * n : (i + 1) * n]


def output(parts, ws):
    n = parts[0].shape[1]
    depth, width = ws[0].shape
    tile = 256
    return pl.pallas_call(
        output_body,
        grid=(2 * width // tile,),
        in_specs=[pl.BlockSpec(parts[0].shape, lambda i: (0, 0, 0))] * 4
        + [
            pl.BlockSpec((depth, tile), lambda i: (0, jnp.minimum(i, 1))),
            pl.BlockSpec((depth, tile), lambda i: (0, jnp.maximum(i - 2, 0))),
        ],
        out_specs=[pl.BlockSpec((n, tile), lambda i: (0, i))] * 4,
        out_shape=[jax.ShapeDtypeStruct((n, 2 * width), BF16)] * 4,
        compiler_params=pltpu.CompilerParams(vmem_limit_bytes=48 << 20),
    )(*parts, *ws)


def place_body(at_ref, x0, x1, x2, x3, out_ref):
    y, c = at_ref[2], at_ref[3]
    width = x0.shape[1]
    for d, x in enumerate((x0, x1, x2, x3)):
        quarter = lax.rem(y - d + N_Y, N_Y)
        for i in range(2):
            eighth = 2 * quarter + (c if i == 0 else 1 - c)
            at = pl.multiple_of(eighth * (width // 2), width // 2)
            out_ref[:, pl.ds(at, width // 2)] = x[:, i * width // 2 : (i + 1) * width // 2]


def place(at, parts):
    rows, width = parts[0].shape
    return pl.pallas_call(
        place_body,
        in_specs=[SMEM] + [VMEM] * 4,
        out_specs=VMEM,
        out_shape=jax.ShapeDtypeStruct((rows, 4 * width), BF16),
    )(at, *parts)


def token_groups():
    groups = []
    for planes in ((0, 2, 5, 7), (1, 3, 4, 6)):
        for y in range(N_Y):
            for c in range(2):
                groups.append([number(x, y, z, c) for x in range(N_X) for z in planes])
    return groups


def shards(tokens, norm_gain, w_qkv, w_out, positions):
    n_uly = lax.axis_size("uly")
    blk, uly = lax.axis_index("blk"), lax.axis_index("uly")
    x, zh = uly // N_Z, uly % N_Z
    z_lo, y, c = blk // 8, (blk // 2) % N_Y, blk % 2
    k = jnp.where(z_lo == 0, zh, 3 - zh)
    at = jnp.stack([x, z_lo, y, c, k]).astype(jnp.int32)
    block_of = positions[::HALF] // HALF

    w = w_qkv[:, 0, :]
    depth = w.shape[0] // 16
    w_part = to_swap(lax.dynamic_slice_in_dim(w, blk * depth, depth, 0))
    w_other = lax.all_gather(w_part, "blk", axis=0, tiled=True)

    normed = norm(tokens, norm_gain)
    mirror = to_mirror(normed)
    own = [normed] + [along_x(normed, d) for d in (-1, 1, 2)]
    far = [mirror] + [along_x(mirror, d) for d in (-1, 1, 2)]
    owns = [partial_product(own, w), partial_product(own, w_other)]

    by_piece = positions.reshape(16, N_X, N_Z, TOK)
    even = lax.dynamic_slice(by_piece, (y * 2 + c, 0, k, 0), (1, N_X, 1, TOK))
    odd = lax.dynamic_slice(by_piece, (8 + y * 2 + c, 0, 3 - k, 0), (1, N_X, 1, TOK))
    cos, sin = rope_tables(jnp.concatenate([even.reshape(-1), odd.reshape(-1)]))
    q, kv, other = project(at, far, [w, w_other], owns, cos, sin)

    eighth = w_out.shape[2] // N_Y // 2
    w_mine = lax.dynamic_slice_in_dim(w_out[0], (blk % 8) * eighth, eighth, 1)
    w_cols = lax.all_gather(after(w_mine, q), "uly", axis=0, tiled=True)

    swapped = to_swap(other)
    kv = jnp.concatenate([kv, swapped[:, HD:]], axis=0)
    q = jnp.concatenate([q, swapped[:, :HD]], axis=0)
    kv_twin = to_twin(kv)
    kv_next, kv_back = along_y(kv, -1), along_y(kv, 1)
    q_parts = [q, to_other_core(q)]
    twin_next, twin_back = along_y(kv_twin, -1), along_y(kv_twin, 1)
    kv_far = [along_y(kv_next[:4], -1), along_y(kv_back[4:], 1)]
    whole, half = (0, 4), (0,)
    state = attend(
        block_of, at, q_parts, None, [(0, [whole, whole])], [kv, kv_twin], False
    )
    twin_next, twin_back = after((twin_next, twin_back), state[2])
    twin_far = [along_y(twin_next[:4], -1), along_y(twin_back[4:], 1)]
    state = attend(
        block_of,
        at,
        None,
        state,
        [(1, [whole, whole]), (-1, [whole, whole])],
        [kv_next, twin_next, kv_back, twin_back],
        False,
    )
    kv_far = after(kv_far, state[2])
    mine, others = attend(
        block_of, at, None, state, [(2, [half] * 4)], kv_far + twin_far, True
    )
    context = merge(at, mine, to_other_core(others))

    w_cols = [w_cols, to_other_core(after(w_cols, context))]
    heads = lax.all_to_all(
        context.reshape(n_uly, TOK, HD), BOTH, 0, 0, axis_index_groups=token_groups()
    )
    rows = [heads] + [along_y(heads, -d) for d in (1, 2, 3)]
    made = output(rows, w_cols)
    parts = [made[0]] + [along_y(made[d], d) for d in (1, 2, 3)]
    return place(at, parts)


def solution(mesh):
    placed = (P(("blk", "uly"), None), P(), P(None, "uly", None), P("uly", None, None), P())
    return jax.shard_map(
        shards, mesh=mesh, in_specs=placed, out_specs=P(("blk", "uly"), None), check_vma=False
    )
```

```python
import functools
import math

import jax
import jax.numpy as jnp
from jax import lax
from jax.experimental import pallas as pl
from jax.experimental.pallas import tpu as pltpu
from jax.sharding import PartitionSpec as P

HALF = 512
HD = 128
LOW = -1e30
EXTRA = 144
N_X, N_Y, N_Z = 4, 4, 4
TOK = 64
SUB = 2 * TOK
BF16 = jnp.bfloat16
F32 = jnp.float32
SMEM = pl.BlockSpec(memory_space=pltpu.SMEM)
VMEM = pl.BlockSpec(memory_space=pltpu.VMEM)
ANY = pl.BlockSpec(memory_space=pl.ANY)
HBM = pl.BlockSpec(memory_space=pltpu.HBM)
BOTH = ("blk", "uly")


def route(move):
    pairs = []
    for x in range(N_X):
        for y in range(N_Y):
            for z in range(2 * N_Z):
                for c in range(2):
                    a, b, d, e = move(x, y, z, c)
                    pairs.append((number(x, y, z, c), number(a % N_X, b % N_Y, d, e)))
    return pairs


def number(x, y, z, c):
    return ((z % 2) * 8 + y * 2 + c) * 16 + x * N_Z + z // 2


def along_x(array, distance):
    return lax.ppermute(array, BOTH, route(lambda x, y, z, c: (x + distance, y, z, c)))


def along_y(array, distance):
    return lax.ppermute(array, BOTH, route(lambda x, y, z, c: (x, y + distance, z, c)))


def to_mirror(array):
    return lax.ppermute(array, BOTH, route(lambda x, y, z, c: (x, y, 7 - z, c)))


def to_swap(array):
    return lax.ppermute(array, BOTH, route(lambda x, y, z, c: (x, y, z ^ 2, c)))


def to_twin(array):
    return lax.ppermute(array, BOTH, route(lambda x, y, z, c: (x, y, z ^ 1, c)))


def to_other_core(array):
    return lax.ppermute(array, BOTH, route(lambda x, y, z, c: (x, y, z, 1 - c)))


def after(values, done):
    return lax.optimization_barrier((values, done))[0]


def rope_tables(places):
    freqs = jnp.exp(jnp.arange(HD // 2, dtype=F32) * (-2.0 * math.log(10000.0) / HD))
    angles = places.astype(F32)[:, None] * freqs[None, :]
    cos, sin = jnp.cos(angles), jnp.sin(angles)
    return jnp.concatenate([cos, cos], 1), jnp.concatenate([-sin, sin], 1)


def norm_body(x_ref, gain_ref, out_ref):
    x = x_ref[...].astype(F32)
    scale = lax.rsqrt(jnp.mean(x * x, axis=-1, keepdims=True) + 1e-05)
    out_ref[...] = (x * scale * gain_ref[...]).astype(BF16)


def norm(tokens, gain, flops=10**6):
    rows, width = tokens.shape
    return pl.pallas_call(
        norm_body,
        in_specs=[VMEM, VMEM],
        out_specs=VMEM,
        out_shape=jax.ShapeDtypeStruct((rows, width), BF16),
        compiler_params=pltpu.CompilerParams(vmem_limit_bytes=12 << 20),
        cost_estimate=pl.CostEstimate(flops=flops, bytes_accessed=1 << 20, transcendentals=0),
    )(tokens, gain.reshape(1, width))


def start_copies(pairs, sems):
    copies = [pltpu.make_async_copy(a, b, sems.at[i]) for i, (a, b) in enumerate(pairs)]
    for copy in copies:
        copy.start()
    return copies


def row_places(refs, buffer):
    pairs, at = [], 0
    for ref in refs:
        pairs.append((ref, buffer.at[at : at + ref.shape[0]]))
        at += ref.shape[0]
    return pairs


def partial_body(*refs):
    x_refs, w_ref, out_ref, rows, sems = refs[:-4], *refs[-4:]
    for copy in start_copies(row_places(x_refs, rows), sems):
        copy.wait()
    out_ref[...] = jnp.dot(rows[...], w_ref[...], preferred_element_type=F32)


def partial_product(arrays, w):
    rows = sum(a.shape[0] for a in arrays)
    return pl.pallas_call(
        partial_body,
        in_specs=[ANY] * len(arrays) + [VMEM],
        out_specs=VMEM,
        out_shape=jax.ShapeDtypeStruct((rows, w.shape[1]), F32),
        scratch_shapes=[
            pltpu.VMEM((rows, w.shape[0]), BF16),
            pltpu.SemaphoreType.DMA((len(arrays),)),
        ],
        compiler_params=pltpu.CompilerParams(vmem_limit_bytes=32 << 20),
        cost_estimate=pl.CostEstimate(
            flops=2 * rows * w.shape[0] * w.shape[1], bytes_accessed=6 << 20, transcendentals=0
        ),
    )(*arrays, w)


def project_body(n_far, at_ref, *refs):
    far_refs, refs = refs[:n_far], refs[n_far:]
    w_refs, own_refs, (cos_ref, sin_ref) = refs[:2], refs[2:4], refs[4:6]
    q_ref, kv_ref, other_ref, rows, packed, sems = refs[6:]
    x, e_own = at_ref[0], at_ref[1]
    for copy in start_copies(row_places(far_refs, rows), sems):
        copy.wait()
    span = N_X * TOK
    for h in range(2):
        far = jnp.dot(rows[...], w_refs[h][...], preferred_element_type=F32)
        for j, dx in enumerate((0, 1, -1, 2)):
            source = lax.rem(x + dx + N_X, N_X) * TOK
            piece = slice(j * TOK, (j + 1) * TOK)
            own_at = pl.ds(pl.multiple_of(e_own * span + source, TOK), TOK)
            far_at = pl.ds(pl.multiple_of((1 - e_own) * span + source, TOK), TOK)
            packed[own_at, :] = own_refs[h][piece, :]
            packed[far_at, :] = far[piece, :]
        for s in range(4):
            at = slice(s * SUB, (s + 1) * SUB)
            cos, sin = cos_ref[at, :], sin_ref[at, :]

            def rot(part):
                return part * cos + pltpu.roll(part, HD // 2, 1) * sin

            query = rot(packed[at, :HD]) * (math.log2(math.e) / math.sqrt(HD))
            query = query.T.astype(BF16)
            key = rot(packed[at, HD : 2 * HD]).astype(BF16)
            value = packed[at, 2 * HD :].T.astype(BF16)
            if h == 0:
                q_ref[s] = query
                kv_ref[s, :SUB] = key
                kv_ref[s, SUB:] = value
            else:
                other_ref[s, :HD] = query
                other_ref[s, HD : HD + SUB] = key
                other_ref[s, HD + SUB :] = value


def project(at, far, ws, owns, cos, sin):
    arrays = [*ws, *owns, cos, sin]
    rows = cos.shape[0]
    shapes = [
        jax.ShapeDtypeStruct((4, HD, SUB), BF16),
        jax.ShapeDtypeStruct((4, 2 * SUB, HD), BF16),
        jax.ShapeDtypeStruct((4, 3 * SUB, HD), BF16),
    ]
    return pl.pallas_call(
        functools.partial(project_body, len(far)),
        in_specs=[SMEM] + [ANY] * len(far) + [VMEM] * len(arrays),
        out_specs=[VMEM] * 3,
        out_shape=shapes,
        scratch_shapes=[
            pltpu.VMEM((rows // 2, far[0].shape[1]), BF16),
            pltpu.VMEM((rows, 3 * HD), F32),
            pltpu.SemaphoreType.DMA((len(far),)),
        ],
        compiler_params=pltpu.CompilerParams(vmem_limit_bytes=32 << 20),
        cost_estimate=pl.CostEstimate(
            flops=rows * 4096 * 6 * HD, bytes_accessed=9 << 20, transcendentals=0
        ),
    )(at, *far, *arrays)


def attend_body(first, last, steps, block_of, at_ref, *refs):
    n_q = 8
    width_q = 2 * SUB
    refs = list(refs)
    take = lambda n: [refs.pop(0) for _ in range(n)]
    n_arrays = 2 * len(steps)
    if first:
        q_parts = take(2)
    else:
        q_sorted, acc_in, top_in = take(3)
    kv_in = take(n_arrays)
    if last:
        outs = take(2)
        acc, top = take(2)
    elif first:
        q_sorted, acc, top = take(3)
    else:
        acc, top = take(2)
    kv_refs = take(n_arrays)
    (sems,) = take(1)
    copies = start_copies(list(zip(kv_in, kv_refs)), sems)

    y, c, k = at_ref[2], at_ref[3], at_ref[4]

    def id_of(e, dy, core, x_hi):
        return block_of[(e * 8 + lax.rem(y + dy + N_Y, N_Y) * 2 + core) * 2 + x_hi]

    q_ids = [id_of(s // 2, 0, core, s % 2) for core in (c, 1 - c) for s in range(4)]
    ranks = [
        functools.reduce(
            jnp.add, [(q_ids[u] < q_ids[v]).astype(jnp.int32) for u in range(n_q) if u != v]
        )
        for v in range(n_q)
    ]
    spots = [pl.ds(pl.multiple_of(rank * width_q, width_q), width_q) for rank in ranks]
    if first:
        for v in range(n_q):
            part, s = q_parts[v // 4], v % 4
            q_sorted[:, spots[v]] = jnp.concatenate([part[s], part[4 + s]], axis=1)
        acc[...] = jnp.zeros_like(acc)
        top[...] = jnp.full_like(top, LOW)
    else:
        acc[...] = acc_in[...]
        top[...] = top_in[...]

    def place_of(index, ks, e):
        run, inside = index // SUB, index % SUB
        at = (inside // TOK) * (N_Z * TOK) + inside % TOK
        for i, kk in enumerate(ks):
            zh = jnp.where(e == 0, kk, 3 - kk)
            at = at + jnp.where(run == i, zh * TOK, 0)
        return at

    other = 3 - k
    key_ks = [k, k ^ 1, other, other ^ 1]

    def tile(load, offset, width):
        cols = slice(offset, offset + width)
        keys, values, e, near, far = load()
        scores = jnp.dot(keys, q_sorted[:, cols], preferred_element_type=F32)
        key_at = place_of(lax.broadcasted_iota(jnp.int32, (HALF, 1), 0), key_ks, e)
        query = lax.broadcasted_iota(jnp.int32, (1, HALF), 1)
        query_at = place_of(query % width_q, key_ks[:2], e)
        reach = jnp.where(query < width_q, near, far)
        head = jnp.where(key_at <= query_at + reach, scores[:, :HALF], LOW)
        scores = head if width == HALF else jnp.concatenate([head, scores[:, HALF:]], axis=1)
        old = top[:1, cols]
        new = jnp.maximum(old, jnp.max(scores, axis=0, keepdims=True))
        weights = jnp.exp2(scores - new).astype(BF16)
        acc[:, cols] = acc[:, cols] * jnp.exp2(old - new) + jnp.dot(
            values, weights, preferred_element_type=F32
        )
        top[:, cols] = jnp.broadcast_to(new, (8, width))

    def key_block(dy, views, s):
        e = s // 2
        block = id_of(e, dy, c, lax.rem(s, 2))
        count = functools.reduce(jnp.add, [(i >= block).astype(jnp.int32) for i in q_ids])
        same = functools.reduce(jnp.add, [(i == block).astype(jnp.int32) for i in q_ids]) > 0
        odd = lax.rem(count, 2) > 0
        edge = jnp.where(same, 0, 2 * HALF)
        near = jnp.where(odd, -2 * HALF, edge)
        far = jnp.where(odd, edge, 2 * HALF)
        pairs = (count + 1) // 2

        def load():
            runs = [ref[base + s] for ref, base in views]
            keys = jnp.concatenate([r[:SUB] for r in runs], axis=0)
            values = jnp.concatenate([r[SUB:] for r in runs], axis=1)
            values = jnp.concatenate([values, jnp.ones((EXTRA - HD, HALF), BF16)], axis=0)
            return keys, values, e, near, far

        for n in range(1, n_q // 2 + 1):

            @pl.when(pairs == n)
            def _(n=n):
                tile(load, (n_q // 2 - n) * HALF, n * HALF)

    for i, dy in enumerate(steps):
        for copy in copies[2 * i : 2 * i + 2]:
            copy.wait()
        views = [(ref, base) for ref in kv_refs[2 * i : 2 * i + 2] for base in (0, 4)]

        @pl.loop(0, 4)
        def _(s, dy=dy, views=views):
            key_block(dy, views, s)

    if last:
        for v in range(n_q):
            total = acc[HD : HD + 1, spots[v]]
            seen = total > 0
            safe = jnp.where(seen, total, 1.0)
            lse = jnp.where(seen, top[:1, spots[v]] + jnp.log2(safe), LOW)
            high = lse.astype(BF16).astype(F32)
            middle = (lse - high).astype(BF16).astype(F32)
            low = lse - high - middle
            row = lax.broadcasted_iota(jnp.int32, (EXTRA - HD, width_q), 0)
            tail = jnp.where(row == 0, high, jnp.where(row == 1, middle, jnp.where(row == 2, low, 0)))
            cols = slice((v % 4) * width_q, (v % 4 + 1) * width_q)
            outs[v // 4][:HD, cols] = (acc[:HD, spots[v]] / safe).astype(BF16)
            outs[v // 4][HD:, cols] = tail.astype(BF16)


def attend(block_of, at, q_parts, state, steps, arrays, last):
    first = state is None
    q_cols = 4 * HALF
    q_shape, acc_shape, top_shape = (HD, q_cols), (EXTRA, q_cols), (8, q_cols)
    args = list(q_parts if first else state) + list(arrays)
    if last:
        out_shape = [jax.ShapeDtypeStruct((EXTRA, q_cols // 2), BF16)] * 2
        scratch = [pltpu.VMEM(acc_shape, F32), pltpu.VMEM(top_shape, F32)]
    else:
        out_shape = [jax.ShapeDtypeStruct(q_shape, BF16)] if first else []
        out_shape += [
            jax.ShapeDtypeStruct(acc_shape, F32),
            jax.ShapeDtypeStruct(top_shape, F32),
        ]
        scratch = []
    scratch += [pltpu.VMEM(a.shape, a.dtype) for a in arrays]
    scratch.append(pltpu.SemaphoreType.DMA((len(arrays),)))
    pairs = 8 * len(steps)
    outs = pl.pallas_call(
        functools.partial(attend_body, first, last, steps),
        in_specs=[SMEM] * 2 + [VMEM] * (len(args) - len(arrays)) + [HBM] * len(arrays),
        out_specs=[VMEM] * len(out_shape),
        out_shape=out_shape,
        scratch_shapes=scratch,
        compiler_params=pltpu.CompilerParams(vmem_limit_bytes=48 << 20),
        cost_estimate=pl.CostEstimate(
            flops=pairs * HALF * HALF * HD * 4,
            bytes_accessed=6 << 20,
            transcendentals=pairs * HALF * HALF,
        ),
    )(block_of, at, *args)
    if last or first:
        return outs
    return [state[0]] + list(outs)


def merge_body(at_ref, own_ref, other_ref, context_ref):
    parts = [own_ref, other_ref]
    lses = []
    for ref in parts:
        tail = ref[HD:, :].astype(F32)
        lses.append(tail[0:1, :] + tail[1:2, :] + tail[2:3, :])
    top = jnp.maximum(*lses)
    shares = [jnp.exp2(lse - top) for lse in lses]
    mixed = [ref[:HD, :].astype(F32) * share for ref, share in zip(parts, shares)]
    context = ((mixed[0] + mixed[1]) / (shares[0] + shares[1])).T.astype(BF16)
    k = at_ref[4]
    for s in range(4):
        for i in range(2):
            kk = k if i == 0 else k ^ 1
            zh = kk if s < 2 else 3 - kk
            for x_lo in range(2):
                x = (s % 2) * 2 + x_lo
                start = (s * 2 + i) * SUB + x_lo * TOK
                at = pl.ds(pl.multiple_of((x * N_Z + zh) * TOK, TOK), TOK)
                context_ref[at, :] = context[start : start + TOK, :]


def merge(at, own, other):
    return pl.pallas_call(
        merge_body,
        in_specs=[SMEM] + [VMEM] * 2,
        out_specs=VMEM,
        out_shape=jax.ShapeDtypeStruct((own.shape[1], HD), BF16),
        compiler_params=pltpu.CompilerParams(vmem_limit_bytes=12 << 20),
    )(at, own, other)


def output_body(x0, x1, x2, x3, w0, w1, o0, o1, o2, o3):
    rows = jnp.concatenate(
        [
            jnp.concatenate([x[h] for h in range(x.shape[0])], axis=1)
            for x in (x0, x1, x2, x3)
        ],
        axis=0,
    )
    w = jnp.where(pl.program_id(0) < 2, w0[...], w1[...])
    out = jnp.dot(rows, w, preferred_element_type=F32).astype(BF16)
    n = x0.shape[1]
    for i, o in enumerate((o0, o1, o2, o3)):
        o[...] = out[i * n : (i + 1) * n]


def output(parts, ws):
    n = parts[0].shape[1]
    depth, width = ws[0].shape
    tile = 256
    return pl.pallas_call(
        output_body,
        grid=(2 * width // tile,),
        in_specs=[pl.BlockSpec(parts[0].shape, lambda i: (0, 0, 0))] * 4
        + [
            pl.BlockSpec((depth, tile), lambda i: (0, jnp.minimum(i, 1))),
            pl.BlockSpec((depth, tile), lambda i: (0, jnp.maximum(i - 2, 0))),
        ],
        out_specs=[pl.BlockSpec((n, tile), lambda i: (0, i))] * 4,
        out_shape=[jax.ShapeDtypeStruct((n, 2 * width), BF16)] * 4,
        compiler_params=pltpu.CompilerParams(vmem_limit_bytes=20 << 20),
    )(*parts, *ws)


def place_body(at_ref, x0, x1, x2, x3, out_ref):
    y, c = at_ref[2], at_ref[3]
    width = x0.shape[1]
    for d, x in enumerate((x0, x1, x2, x3)):
        quarter = lax.rem(y - d + N_Y, N_Y)
        for i in range(2):
            eighth = 2 * quarter + (c if i == 0 else 1 - c)
            at = pl.multiple_of(eighth * (width // 2), width // 2)
            out_ref[:, pl.ds(at, width // 2)] = x[:, i * width // 2 : (i + 1) * width // 2]


def place(at, parts):
    rows, width = parts[0].shape
    return pl.pallas_call(
        place_body,
        in_specs=[SMEM] + [VMEM] * 4,
        out_specs=VMEM,
        out_shape=jax.ShapeDtypeStruct((rows, 4 * width), BF16),
        compiler_params=pltpu.CompilerParams(vmem_limit_bytes=12 << 20),
    )(at, *parts)


def token_groups():
    groups = []
    for planes in ((0, 2, 5, 7), (1, 3, 4, 6)):
        for y in range(N_Y):
            for c in range(2):
                groups.append([number(x, y, z, c) for x in range(N_X) for z in planes])
    return groups


def shards(tokens, norm_gain, w_qkv, w_out, positions):
    n_uly = lax.axis_size("uly")
    blk, uly = lax.axis_index("blk"), lax.axis_index("uly")
    x, zh = uly // N_Z, uly % N_Z
    z_lo, y, c = blk // 8, (blk // 2) % N_Y, blk % 2
    k = jnp.where(z_lo == 0, zh, 3 - zh)
    at = jnp.stack([x, z_lo, y, c, k]).astype(jnp.int32)
    block_of = positions[::HALF] // HALF

    w = w_qkv[:, 0, :]
    depth = w.shape[0] // 8
    w_part = to_swap(lax.dynamic_slice_in_dim(w, (blk % 8) * depth, depth, 0))
    mirror = to_mirror(tokens)
    normed = norm(tokens, norm_gain)
    own = [normed] + [along_x(normed, d) for d in (-1, 1, 2)]
    w_part = after(w_part, (mirror, own))
    same_z = [list(range(8)), list(range(8, 16))]
    w_other = lax.all_gather(w_part, "blk", axis_index_groups=same_z, axis=0, tiled=True)
    mirror = norm(mirror, norm_gain)
    far = [mirror] + [along_x(mirror, d) for d in (-1, 1, 2)]
    owns = [partial_product(own, w), partial_product(own, w_other)]

    by_piece = positions.reshape(16, N_X, N_Z, TOK)
    even = lax.dynamic_slice(by_piece, (y * 2 + c, 0, k, 0), (1, N_X, 1, TOK))
    odd = lax.dynamic_slice(by_piece, (8 + y * 2 + c, 0, 3 - k, 0), (1, N_X, 1, TOK))
    cos, sin = rope_tables(jnp.concatenate([even.reshape(-1), odd.reshape(-1)]))
    q, kv, other = project(at, far, [w, w_other], owns, cos, sin)

    swapped = to_swap(other)
    eighth = w_out.shape[2] // N_Y // 2
    w_mine = lax.dynamic_slice_in_dim(w_out[0], (blk % 8) * eighth, eighth, 1)
    w_cols = lax.all_gather(after(w_mine, swapped), "uly", axis=0, tiled=True)

    kv = jnp.concatenate([kv, swapped[:, HD:]], axis=0)
    q = jnp.concatenate([q, swapped[:, :HD]], axis=0)
    kv_twin = to_twin(kv)
    kv_next, kv_back = along_y(kv, -1), along_y(kv, 1)
    qs = [q, to_other_core(q)]
    kv_twin = after(kv_twin, (qs[1], kv_next, kv_back))

    twin_next, twin_back = along_y(kv_twin, -1), along_y(kv_twin, 1)
    state = attend(block_of, at, qs, None, [0], [kv, kv_twin], False)
    twin_next, twin_back = after((twin_next, twin_back), state[2])
    kv_far = along_y(after(kv_next, (twin_next, twin_back)), -1)
    twin_far = along_y(twin_back, 1)
    state = attend(
        block_of, at, None, state, [1, -1], [kv_next, twin_next, kv_back, twin_back], False
    )
    mine, others = attend(block_of, at, None, state, [2], [kv_far, twin_far], True)
    context = merge(at, mine, to_other_core(others))

    heads = lax.all_to_all(
        context.reshape(n_uly, TOK, HD), BOTH, 0, 0, axis_index_groups=token_groups()
    )
    w_cols = [w_cols, to_other_core(after(w_cols, heads))]
    rows = [heads] + [along_y(heads, -d) for d in (1, 2, 3)]
    made = output(rows, w_cols)
    parts = [made[0]] + [along_y(made[d], d) for d in (1, 2, 3)]
    return place(at, parts)


def solution(mesh):
    placed = (P(("blk", "uly"), None), P(), P(None, "uly", None), P("uly", None, None), P())
    return jax.shard_map(
        shards, mesh=mesh, in_specs=placed, out_specs=P(("blk", "uly"), None), check_vma=False
    )
```

```python
import functools
import math

import jax
import jax.numpy as jnp
from jax import lax
from jax.experimental import pallas as pl
from jax.experimental.pallas import tpu as pltpu
from jax.sharding import PartitionSpec as P

HALF = 512
HD = 128
LOW = -1e30
EXTRA = 144
N_X, N_Y, N_Z = 4, 4, 4
TOK = 64
SUB = 2 * TOK
BF16 = jnp.bfloat16
F32 = jnp.float32
SMEM = pl.BlockSpec(memory_space=pltpu.SMEM)
VMEM = pl.BlockSpec(memory_space=pltpu.VMEM)
ANY = pl.BlockSpec(memory_space=pl.ANY)
HBM = pl.BlockSpec(memory_space=pltpu.HBM)
BOTH = ("blk", "uly")


def route(move):
    pairs = []
    for x in range(N_X):
        for y in range(N_Y):
            for z in range(2 * N_Z):
                for c in range(2):
                    a, b, d, e = move(x, y, z, c)
                    pairs.append((number(x, y, z, c), number(a % N_X, b % N_Y, d, e)))
    return pairs


def number(x, y, z, c):
    return ((z % 2) * 8 + y * 2 + c) * 16 + x * N_Z + z // 2


def along_x(array, distance):
    return lax.ppermute(array, BOTH, route(lambda x, y, z, c: (x + distance, y, z, c)))


def along_y(array, distance):
    return lax.ppermute(array, BOTH, route(lambda x, y, z, c: (x, y + distance, z, c)))


def to_mirror(array):
    return lax.ppermute(array, BOTH, route(lambda x, y, z, c: (x, y, 7 - z, c)))


def to_swap(array):
    return lax.ppermute(array, BOTH, route(lambda x, y, z, c: (x, y, z ^ 2, c)))


def to_twin(array):
    return lax.ppermute(array, BOTH, route(lambda x, y, z, c: (x, y, z ^ 1, c)))


def to_other_core(array):
    return lax.ppermute(array, BOTH, route(lambda x, y, z, c: (x, y, z, 1 - c)))


def after(values, done):
    return lax.optimization_barrier((values, done))[0]


def rope_tables(places):
    freqs = jnp.exp(jnp.arange(HD // 2, dtype=F32) * (-2.0 * math.log(10000.0) / HD))
    angles = places.astype(F32)[:, None] * freqs[None, :]
    cos, sin = jnp.cos(angles), jnp.sin(angles)
    return jnp.concatenate([cos, cos], 1), jnp.concatenate([-sin, sin], 1)


def norm_body(x_ref, gain_ref, out_ref):
    x = x_ref[...].astype(F32)
    scale = lax.rsqrt(jnp.mean(x * x, axis=-1, keepdims=True) + 1e-05)
    out_ref[...] = (x * scale * gain_ref[...]).astype(BF16)


def norm(tokens, gain, flops=10**6):
    rows, width = tokens.shape
    return pl.pallas_call(
        norm_body,
        in_specs=[VMEM, VMEM],
        out_specs=VMEM,
        out_shape=jax.ShapeDtypeStruct((rows, width), BF16),
        compiler_params=pltpu.CompilerParams(vmem_limit_bytes=12 << 20),
        cost_estimate=pl.CostEstimate(flops=flops, bytes_accessed=1 << 20, transcendentals=0),
    )(tokens, gain.reshape(1, width))


def start_copies(pairs, sems):
    copies = [pltpu.make_async_copy(a, b, sems.at[i]) for i, (a, b) in enumerate(pairs)]
    for copy in copies:
        copy.start()
    return copies


def row_places(refs, buffer):
    pairs, at = [], 0
    for ref in refs:
        pairs.append((ref, buffer.at[at : at + ref.shape[0]]))
        at += ref.shape[0]
    return pairs


def partial_body(*refs):
    x_refs, w_ref, out_ref, rows, sems = refs[:-4], *refs[-4:]
    for copy in start_copies(row_places(x_refs, rows), sems):
        copy.wait()
    out_ref[...] = jnp.dot(rows[...], w_ref[...], preferred_element_type=F32)


def partial_product(arrays, w):
    rows = sum(a.shape[0] for a in arrays)
    return pl.pallas_call(
        partial_body,
        in_specs=[ANY] * len(arrays) + [VMEM],
        out_specs=VMEM,
        out_shape=jax.ShapeDtypeStruct((rows, w.shape[1]), F32),
        scratch_shapes=[
            pltpu.VMEM((rows, w.shape[0]), BF16),
            pltpu.SemaphoreType.DMA((len(arrays),)),
        ],
        compiler_params=pltpu.CompilerParams(vmem_limit_bytes=32 << 20),
        cost_estimate=pl.CostEstimate(
            flops=2 * rows * w.shape[0] * w.shape[1], bytes_accessed=6 << 20, transcendentals=0
        ),
    )(*arrays, w)


def project_body(n_far, at_ref, *refs):
    far_refs, refs = refs[:n_far], refs[n_far:]
    w_refs, own_refs, (cos_ref, sin_ref) = refs[:2], refs[2:4], refs[4:6]
    q_ref, kv_ref, other_q_ref, other_kv_ref, rows, packed, sems = refs[6:]
    x, e_own = at_ref[0], at_ref[1]
    for copy in start_copies(row_places(far_refs, rows), sems):
        copy.wait()
    span = N_X * TOK
    for h in range(2):
        far = jnp.dot(rows[...], w_refs[h][...], preferred_element_type=F32)
        for j, dx in enumerate((0, 1, -1, 2)):
            source = lax.rem(x + dx + N_X, N_X) * TOK
            piece = slice(j * TOK, (j + 1) * TOK)
            own_at = pl.ds(pl.multiple_of(e_own * span + source, TOK), TOK)
            far_at = pl.ds(pl.multiple_of((1 - e_own) * span + source, TOK), TOK)
            packed[own_at, :] = own_refs[h][piece, :]
            packed[far_at, :] = far[piece, :]
        for s in range(4):
            at = slice(s * SUB, (s + 1) * SUB)
            cos, sin = cos_ref[at, :], sin_ref[at, :]

            def rot(part):
                return part * cos + pltpu.roll(part, HD // 2, 1) * sin

            query = rot(packed[at, :HD]) * (math.log2(math.e) / math.sqrt(HD))
            query = query.T.astype(BF16)
            key = rot(packed[at, HD : 2 * HD]).astype(BF16)
            value = packed[at, 2 * HD :].T.astype(BF16)
            q_out, kv_out = (q_ref, kv_ref) if h == 0 else (other_q_ref, other_kv_ref)
            q_out[s] = query
            kv_out[s, :SUB] = key
            kv_out[s, SUB:] = value


def project(at, far, ws, owns, cos, sin):
    arrays = [*ws, *owns, cos, sin]
    rows = cos.shape[0]
    shapes = [
        jax.ShapeDtypeStruct((4, HD, SUB), BF16),
        jax.ShapeDtypeStruct((4, 2 * SUB, HD), BF16),
    ]
    return pl.pallas_call(
        functools.partial(project_body, len(far)),
        in_specs=[SMEM] + [ANY] * len(far) + [VMEM] * len(arrays),
        out_specs=[VMEM] * 4,
        out_shape=shapes * 2,
        scratch_shapes=[
            pltpu.VMEM((rows // 2, far[0].shape[1]), BF16),
            pltpu.VMEM((rows, 3 * HD), F32),
            pltpu.SemaphoreType.DMA((len(far),)),
        ],
        compiler_params=pltpu.CompilerParams(vmem_limit_bytes=32 << 20),
        cost_estimate=pl.CostEstimate(
            flops=rows * 4096 * 6 * HD, bytes_accessed=9 << 20, transcendentals=0
        ),
    )(at, *far, *arrays)


def attend_body(first, last, steps, block_of, at_ref, *refs):
    n_q = 8
    width_q = 2 * SUB
    refs = list(refs)
    take = lambda n: [refs.pop(0) for _ in range(n)]
    n_arrays = 2 * len(steps)
    if first:
        q_parts = take(2)
    else:
        q_sorted, acc_in, top_in = take(3)
    kv_in = take(n_arrays)
    if last:
        outs = take(2)
        acc, top = take(2)
    elif first:
        q_sorted, acc, top = take(3)
    else:
        acc, top = take(2)
    kv_refs = take(n_arrays)
    (sems,) = take(1)
    copies = start_copies(list(zip(kv_in, kv_refs)), sems)

    y, c, k = at_ref[2], at_ref[3], at_ref[4]

    def id_of(e, dy, core, x_hi):
        return block_of[(e * 8 + lax.rem(y + dy + N_Y, N_Y) * 2 + core) * 2 + x_hi]

    q_ids = [id_of(s // 2, 0, core, s % 2) for core in (c, 1 - c) for s in range(4)]
    ranks = [
        functools.reduce(
            jnp.add, [(q_ids[u] < q_ids[v]).astype(jnp.int32) for u in range(n_q) if u != v]
        )
        for v in range(n_q)
    ]
    spots = [pl.ds(pl.multiple_of(rank * width_q, width_q), width_q) for rank in ranks]
    if first:
        for v in range(n_q):
            part, s = q_parts[v // 4], v % 4
            q_sorted[:, spots[v]] = jnp.concatenate([part[s], part[4 + s]], axis=1)
        acc[...] = jnp.zeros_like(acc)
        top[...] = jnp.full_like(top, LOW)
    else:
        acc[...] = acc_in[...]
        top[...] = top_in[...]

    def place_of(index, ks, e):
        run, inside = index // SUB, index % SUB
        at = (inside // TOK) * (N_Z * TOK) + inside % TOK
        for i, kk in enumerate(ks):
            zh = jnp.where(e == 0, kk, 3 - kk)
            at = at + jnp.where(run == i, zh * TOK, 0)
        return at

    other = 3 - k
    key_ks = [k, k ^ 1, other, other ^ 1]

    def tile(load, offset, width):
        cols = slice(offset, offset + width)
        keys, values, e, near, far = load()
        scores = jnp.dot(keys, q_sorted[:, cols], preferred_element_type=F32)
        key_at = place_of(lax.broadcasted_iota(jnp.int32, (HALF, 1), 0), key_ks, e)
        query = lax.broadcasted_iota(jnp.int32, (1, HALF), 1)
        query_at = place_of(query % width_q, key_ks[:2], e)
        reach = jnp.where(query < width_q, near, far)
        head = jnp.where(key_at <= query_at + reach, scores[:, :HALF], LOW)
        scores = head if width == HALF else jnp.concatenate([head, scores[:, HALF:]], axis=1)
        old = top[:1, cols]
        new = jnp.maximum(old, jnp.max(scores, axis=0, keepdims=True))
        weights = jnp.exp2(scores - new).astype(BF16)
        acc[:, cols] = acc[:, cols] * jnp.exp2(old - new) + jnp.dot(
            values, weights, preferred_element_type=F32
        )
        top[:, cols] = jnp.broadcast_to(new, (8, width))

    def key_block(dy, views, s):
        e = s // 2
        block = id_of(e, dy, c, lax.rem(s, 2))
        count = functools.reduce(jnp.add, [(i >= block).astype(jnp.int32) for i in q_ids])
        same = functools.reduce(jnp.add, [(i == block).astype(jnp.int32) for i in q_ids]) > 0
        odd = lax.rem(count, 2) > 0
        edge = jnp.where(same, 0, 2 * HALF)
        near = jnp.where(odd, -2 * HALF, edge)
        far = jnp.where(odd, edge, 2 * HALF)
        pairs = (count + 1) // 2

        def load():
            runs = [ref[base + s] for ref, base in views]
            keys = jnp.concatenate([r[:SUB] for r in runs], axis=0)
            values = jnp.concatenate([r[SUB:] for r in runs], axis=1)
            values = jnp.concatenate([values, jnp.ones((EXTRA - HD, HALF), BF16)], axis=0)
            return keys, values, e, near, far

        for n in range(1, n_q // 2 + 1):

            @pl.when(pairs == n)
            def _(n=n):
                tile(load, (n_q // 2 - n) * HALF, n * HALF)

    for i, dy in enumerate(steps):
        for copy in copies[2 * i : 2 * i + 2]:
            copy.wait()
        views = [(ref, base) for ref in kv_refs[2 * i : 2 * i + 2] for base in (0, 4)]

        @pl.loop(0, 4)
        def _(s, dy=dy, views=views):
            key_block(dy, views, s)

    if last:
        for v in range(n_q):
            total = acc[HD : HD + 1, spots[v]]
            seen = total > 0
            safe = jnp.where(seen, total, 1.0)
            lse = jnp.where(seen, top[:1, spots[v]] + jnp.log2(safe), LOW)
            high = lse.astype(BF16).astype(F32)
            middle = (lse - high).astype(BF16).astype(F32)
            low = lse - high - middle
            row = lax.broadcasted_iota(jnp.int32, (EXTRA - HD, width_q), 0)
            tail = jnp.where(row == 0, high, jnp.where(row == 1, middle, jnp.where(row == 2, low, 0)))
            cols = slice((v % 4) * width_q, (v % 4 + 1) * width_q)
            outs[v // 4][:HD, cols] = (acc[:HD, spots[v]] / safe).astype(BF16)
            outs[v // 4][HD:, cols] = tail.astype(BF16)


def attend(block_of, at, q_parts, state, steps, arrays, last):
    first = state is None
    q_cols = 4 * HALF
    q_shape, acc_shape, top_shape = (HD, q_cols), (EXTRA, q_cols), (8, q_cols)
    args = list(q_parts if first else state) + list(arrays)
    if last:
        out_shape = [jax.ShapeDtypeStruct((EXTRA, q_cols // 2), BF16)] * 2
        scratch = [pltpu.VMEM(acc_shape, F32), pltpu.VMEM(top_shape, F32)]
    else:
        out_shape = [jax.ShapeDtypeStruct(q_shape, BF16)] if first else []
        out_shape += [
            jax.ShapeDtypeStruct(acc_shape, F32),
            jax.ShapeDtypeStruct(top_shape, F32),
        ]
        scratch = []
    scratch += [pltpu.VMEM(a.shape, a.dtype) for a in arrays]
    scratch.append(pltpu.SemaphoreType.DMA((len(arrays),)))
    pairs = 8 * len(steps)
    outs = pl.pallas_call(
        functools.partial(attend_body, first, last, steps),
        in_specs=[SMEM] * 2 + [VMEM] * (len(args) - len(arrays)) + [HBM] * len(arrays),
        out_specs=[VMEM] * len(out_shape),
        out_shape=out_shape,
        scratch_shapes=scratch,
        compiler_params=pltpu.CompilerParams(vmem_limit_bytes=48 << 20),
        cost_estimate=pl.CostEstimate(
            flops=pairs * HALF * HALF * HD * 4,
            bytes_accessed=6 << 20,
            transcendentals=pairs * HALF * HALF,
        ),
    )(block_of, at, *args)
    if last or first:
        return outs
    return [state[0]] + list(outs)


def merge_body(at_ref, own_ref, other_ref, context_ref):
    parts = [own_ref, other_ref]
    lses = []
    for ref in parts:
        tail = ref[HD:, :].astype(F32)
        lses.append(tail[0:1, :] + tail[1:2, :] + tail[2:3, :])
    top = jnp.maximum(*lses)
    shares = [jnp.exp2(lse - top) for lse in lses]
    mixed = [ref[:HD, :].astype(F32) * share for ref, share in zip(parts, shares)]
    context = ((mixed[0] + mixed[1]) / (shares[0] + shares[1])).T.astype(BF16)
    k = at_ref[4]
    for s in range(4):
        for i in range(2):
            kk = k if i == 0 else k ^ 1
            zh = kk if s < 2 else 3 - kk
            for x_lo in range(2):
                x = (s % 2) * 2 + x_lo
                start = (s * 2 + i) * SUB + x_lo * TOK
                at = pl.ds(pl.multiple_of((x * N_Z + zh) * TOK, TOK), TOK)
                context_ref[at, :] = context[start : start + TOK, :]


def merge(at, own, other):
    return pl.pallas_call(
        merge_body,
        in_specs=[SMEM] + [VMEM] * 2,
        out_specs=VMEM,
        out_shape=jax.ShapeDtypeStruct((own.shape[1], HD), BF16),
        compiler_params=pltpu.CompilerParams(vmem_limit_bytes=12 << 20),
    )(at, own, other)


def output_body(x0, x1, x2, x3, w0, w1, o0, o1, o2, o3):
    rows = jnp.concatenate(
        [
            jnp.concatenate([x[h] for h in range(x.shape[0])], axis=1)
            for x in (x0, x1, x2, x3)
        ],
        axis=0,
    )
    w = jnp.where(pl.program_id(0) < 2, w0[...], w1[...])
    out = jnp.dot(rows, w, preferred_element_type=F32).astype(BF16)
    n = x0.shape[1]
    for i, o in enumerate((o0, o1, o2, o3)):
        o[...] = out[i * n : (i + 1) * n]


def output(parts, ws):
    n = parts[0].shape[1]
    depth, width = ws[0].shape
    tile = 256
    return pl.pallas_call(
        output_body,
        grid=(2 * width // tile,),
        in_specs=[pl.BlockSpec(parts[0].shape, lambda i: (0, 0, 0))] * 4
        + [
            pl.BlockSpec((depth, tile), lambda i: (0, jnp.minimum(i, 1))),
            pl.BlockSpec((depth, tile), lambda i: (0, jnp.maximum(i - 2, 0))),
        ],
        out_specs=[pl.BlockSpec((n, tile), lambda i: (0, i))] * 4,
        out_shape=[jax.ShapeDtypeStruct((n, 2 * width), BF16)] * 4,
        compiler_params=pltpu.CompilerParams(vmem_limit_bytes=20 << 20),
    )(*parts, *ws)


def place_body(at_ref, x0, x1, x2, x3, out_ref):
    y, c = at_ref[2], at_ref[3]
    width = x0.shape[1]
    for d, x in enumerate((x0, x1, x2, x3)):
        quarter = lax.rem(y - d + N_Y, N_Y)
        for i in range(2):
            eighth = 2 * quarter + (c if i == 0 else 1 - c)
            at = pl.multiple_of(eighth * (width // 2), width // 2)
            out_ref[:, pl.ds(at, width // 2)] = x[:, i * width // 2 : (i + 1) * width // 2]


def place(at, parts):
    rows, width = parts[0].shape
    return pl.pallas_call(
        place_body,
        in_specs=[SMEM] + [VMEM] * 4,
        out_specs=VMEM,
        out_shape=jax.ShapeDtypeStruct((rows, 4 * width), BF16),
        compiler_params=pltpu.CompilerParams(vmem_limit_bytes=12 << 20),
    )(at, *parts)


def token_groups():
    groups = []
    for planes in ((0, 2, 5, 7), (1, 3, 4, 6)):
        for y in range(N_Y):
            for c in range(2):
                groups.append([number(x, y, z, c) for x in range(N_X) for z in planes])
    return groups


def shards(tokens, norm_gain, w_qkv, w_out, positions):
    n_uly = lax.axis_size("uly")
    blk, uly = lax.axis_index("blk"), lax.axis_index("uly")
    x, zh = uly // N_Z, uly % N_Z
    z_lo, y, c = blk // 8, (blk // 2) % N_Y, blk % 2
    k = jnp.where(z_lo == 0, zh, 3 - zh)
    at = jnp.stack([x, z_lo, y, c, k]).astype(jnp.int32)
    block_of = positions[::HALF] // HALF

    w = w_qkv[:, 0, :]
    depth = w.shape[0] // 8
    w_part = to_swap(lax.dynamic_slice_in_dim(w, (blk % 8) * depth, depth, 0))
    mirror = to_mirror(tokens)
    normed = norm(tokens, norm_gain)
    own = [normed] + [along_x(normed, d) for d in (-1, 1, 2)]
    w_part = after(w_part, (mirror, own))
    same_z = [list(range(8)), list(range(8, 16))]
    w_other = lax.all_gather(w_part, "blk", axis_index_groups=same_z, axis=0, tiled=True)
    mirror = norm(mirror, norm_gain)
    far = [mirror] + [along_x(mirror, d) for d in (-1, 1, 2)]
    owns = [partial_product(own, w), partial_product(own, w_other)]

    by_piece = positions.reshape(16, N_X, N_Z, TOK)
    even = lax.dynamic_slice(by_piece, (y * 2 + c, 0, k, 0), (1, N_X, 1, TOK))
    odd = lax.dynamic_slice(by_piece, (8 + y * 2 + c, 0, 3 - k, 0), (1, N_X, 1, TOK))
    cos, sin = rope_tables(jnp.concatenate([even.reshape(-1), odd.reshape(-1)]))
    q, kv, other_q, other_kv = project(at, far, [w, w_other], owns, cos, sin)

    swapped, swapped_q = to_swap(other_kv), to_swap(other_q)
    eighth = w_out.shape[2] // N_Y // 2
    w_mine = lax.dynamic_slice_in_dim(w_out[0], (blk % 8) * eighth, eighth, 1)
    w_cols = lax.all_gather(after(w_mine, swapped), "uly", axis=0, tiled=True)

    kv = jnp.concatenate([kv, swapped], axis=0)
    q = jnp.concatenate([q, swapped_q], axis=0)
    kv_twin = to_twin(kv)
    kv_next, kv_back = along_y(kv, -1), along_y(kv, 1)
    qs = [q, to_other_core(q)]
    kv_twin = after(kv_twin, (kv_next, kv_back))

    twin_next, twin_back = along_y(kv_twin, -1), along_y(kv_twin, 1)
    state = attend(block_of, at, qs, None, [0], [kv, kv_twin], False)
    twin_next, twin_back = after((twin_next, twin_back), state[2])
    kv_far = along_y(after(kv_next, (twin_next, twin_back)), -1)
    twin_far = along_y(twin_back, 1)
    state = attend(
        block_of, at, None, state, [1, -1], [kv_next, twin_next, kv_back, twin_back], False
    )
    mine, others = attend(block_of, at, None, state, [2], [kv_far, twin_far], True)
    context = merge(at, mine, to_other_core(others))

    heads = lax.all_to_all(
        context.reshape(n_uly, TOK, HD), BOTH, 0, 0, axis_index_groups=token_groups()
    )
    w_cols = [w_cols, to_other_core(after(w_cols, heads))]
    rows = [heads] + [along_y(heads, -d) for d in (1, 2, 3)]
    made = output(rows, w_cols)
    parts = [made[0]] + [along_y(made[d], d) for d in (1, 2, 3)]
    return place(at, parts)


def solution(mesh):
    placed = (P(("blk", "uly"), None), P(), P(None, "uly", None), P("uly", None, None), P())
    return jax.shard_map(
        shards, mesh=mesh, in_specs=placed, out_specs=P(("blk", "uly"), None), check_vma=False
    )
```

```python
import functools
import math

import jax
import jax.numpy as jnp
from jax import lax
from jax.experimental import pallas as pl
from jax.experimental.pallas import tpu as pltpu
from jax.sharding import PartitionSpec as P

HALF = 512
HD = 128
LOW = -1e30
EXTRA = 144
N_X, N_Y, N_Z = 4, 4, 4
TOK = 64
SUB = 2 * TOK
BF16 = jnp.bfloat16
F32 = jnp.float32
SMEM = pl.BlockSpec(memory_space=pltpu.SMEM)
VMEM = pl.BlockSpec(memory_space=pltpu.VMEM)
ANY = pl.BlockSpec(memory_space=pl.ANY)
HBM = pl.BlockSpec(memory_space=pltpu.HBM)
BOTH = ("blk", "uly")


def route(move):
    pairs = []
    for x in range(N_X):
        for y in range(N_Y):
            for z in range(2 * N_Z):
                for c in range(2):
                    a, b, d, e = move(x, y, z, c)
                    pairs.append((number(x, y, z, c), number(a % N_X, b % N_Y, d, e)))
    return pairs


def number(x, y, z, c):
    return ((z % 2) * 8 + y * 2 + c) * 16 + x * N_Z + z // 2


def along_x(array, distance):
    return lax.ppermute(array, BOTH, route(lambda x, y, z, c: (x + distance, y, z, c)))


def along_y(array, distance):
    return lax.ppermute(array, BOTH, route(lambda x, y, z, c: (x, y + distance, z, c)))


def to_mirror(array):
    return lax.ppermute(array, BOTH, route(lambda x, y, z, c: (x, y, 7 - z, c)))


def to_swap(array):
    return lax.ppermute(array, BOTH, route(lambda x, y, z, c: (x, y, z ^ 2, c)))


def to_swap_across(array):
    return lax.ppermute(array, BOTH, route(lambda x, y, z, c: (x, y, z ^ 2, 1 - c)))


def to_twin(array):
    return lax.ppermute(array, BOTH, route(lambda x, y, z, c: (x, y, z ^ 1, c)))


def to_other_core(array):
    return lax.ppermute(array, BOTH, route(lambda x, y, z, c: (x, y, z, 1 - c)))


def after(values, done):
    return lax.optimization_barrier((values, done))[0]


def rope_tables(places):
    freqs = jnp.exp(jnp.arange(HD // 2, dtype=F32) * (-2.0 * math.log(10000.0) / HD))
    angles = places.astype(F32)[:, None] * freqs[None, :]
    cos, sin = jnp.cos(angles), jnp.sin(angles)
    return jnp.concatenate([cos, cos], 1), jnp.concatenate([-sin, sin], 1)


def norm_body(x_ref, gain_ref, out_ref):
    x = x_ref[...].astype(F32)
    scale = lax.rsqrt(jnp.mean(x * x, axis=-1, keepdims=True) + 1e-05)
    out_ref[...] = (x * scale * gain_ref[...]).astype(BF16)


def norm(tokens, gain, flops=10**6):
    rows, width = tokens.shape
    return pl.pallas_call(
        norm_body,
        in_specs=[VMEM, VMEM],
        out_specs=VMEM,
        out_shape=jax.ShapeDtypeStruct((rows, width), BF16),
        compiler_params=pltpu.CompilerParams(vmem_limit_bytes=12 << 20),
        cost_estimate=pl.CostEstimate(flops=flops, bytes_accessed=1 << 20, transcendentals=0),
    )(tokens, gain.reshape(1, width))


def start_copies(pairs, sems):
    copies = [pltpu.make_async_copy(a, b, sems.at[i]) for i, (a, b) in enumerate(pairs)]
    for copy in copies:
        copy.start()
    return copies


def row_places(refs, buffer):
    pairs, at = [], 0
    for ref in refs:
        pairs.append((ref, buffer.at[at : at + ref.shape[0]]))
        at += ref.shape[0]
    return pairs


def partial_body(*refs):
    x_refs, w_ref, out_ref, rows, sems = refs[:-4], *refs[-4:]
    for copy in start_copies(row_places(x_refs, rows), sems):
        copy.wait()
    out_ref[...] = jnp.dot(rows[...], w_ref[...], preferred_element_type=F32)


def partial_product(arrays, w):
    rows = sum(a.shape[0] for a in arrays)
    return pl.pallas_call(
        partial_body,
        in_specs=[ANY] * len(arrays) + [VMEM],
        out_specs=VMEM,
        out_shape=jax.ShapeDtypeStruct((rows, w.shape[1]), F32),
        scratch_shapes=[
            pltpu.VMEM((rows, w.shape[0]), BF16),
            pltpu.SemaphoreType.DMA((len(arrays),)),
        ],
        compiler_params=pltpu.CompilerParams(vmem_limit_bytes=32 << 20),
        cost_estimate=pl.CostEstimate(
            flops=2 * rows * w.shape[0] * w.shape[1], bytes_accessed=6 << 20, transcendentals=0
        ),
    )(*arrays, w)


def project_body(n_far, at_ref, *refs):
    far_refs, refs = refs[:n_far], refs[n_far:]
    w_refs, own_refs, (cos_ref, sin_ref) = refs[:2], refs[2:4], refs[4:6]
    q_ref, kv_ref, other_q_ref, other_kv_ref, rows, packed, sems = refs[6:]
    x, e_own = at_ref[0], at_ref[1]
    for copy in start_copies(row_places(far_refs, rows), sems):
        copy.wait()
    span = N_X * TOK
    for h in range(2):
        far = jnp.dot(rows[...], w_refs[h][...], preferred_element_type=F32)
        for j, dx in enumerate((0, 1, -1, 2)):
            source = lax.rem(x + dx + N_X, N_X) * TOK
            piece = slice(j * TOK, (j + 1) * TOK)
            own_at = pl.ds(pl.multiple_of(e_own * span + source, TOK), TOK)
            far_at = pl.ds(pl.multiple_of((1 - e_own) * span + source, TOK), TOK)
            packed[own_at, :] = own_refs[h][piece, :]
            packed[far_at, :] = far[piece, :]
        for s in range(4):
            at = slice(s * SUB, (s + 1) * SUB)
            cos, sin = cos_ref[at, :], sin_ref[at, :]

            def rot(part):
                return part * cos + pltpu.roll(part, HD // 2, 1) * sin

            query = rot(packed[at, :HD]) * (math.log2(math.e) / math.sqrt(HD))
            query = query.T.astype(BF16)
            key = rot(packed[at, HD : 2 * HD]).astype(BF16)
            value = packed[at, 2 * HD :].T.astype(BF16)
            q_out, kv_out = (q_ref, kv_ref) if h == 0 else (other_q_ref, other_kv_ref)
            q_out[s] = query
            kv_out[s, :SUB] = key
            kv_out[s, SUB:] = value


def project(at, far, ws, owns, cos, sin):
    arrays = [*ws, *owns, cos, sin]
    rows = cos.shape[0]
    shapes = [
        jax.ShapeDtypeStruct((4, HD, SUB), BF16),
        jax.ShapeDtypeStruct((4, 2 * SUB, HD), BF16),
    ]
    return pl.pallas_call(
        functools.partial(project_body, len(far)),
        in_specs=[SMEM] + [ANY] * len(far) + [VMEM] * len(arrays),
        out_specs=[VMEM] * 4,
        out_shape=shapes * 2,
        scratch_shapes=[
            pltpu.VMEM((rows // 2, far[0].shape[1]), BF16),
            pltpu.VMEM((rows, 3 * HD), F32),
            pltpu.SemaphoreType.DMA((len(far),)),
        ],
        compiler_params=pltpu.CompilerParams(vmem_limit_bytes=32 << 20),
        cost_estimate=pl.CostEstimate(
            flops=rows * 4096 * 6 * HD, bytes_accessed=9 << 20, transcendentals=0
        ),
    )(at, *far, *arrays)


def attend_body(first, last, steps, block_of, at_ref, *refs):
    n_q = 8
    width_q = 2 * SUB
    refs = list(refs)
    take = lambda n: [refs.pop(0) for _ in range(n)]
    n_arrays = 2 * len(steps)
    if first:
        q_parts = take(4)
    else:
        q_sorted, acc_in, top_in = take(3)
    kv_in = take(n_arrays)
    if last:
        outs = take(2)
        acc, top = take(2)
    elif first:
        q_sorted, acc, top = take(3)
    else:
        acc, top = take(2)
    kv_refs = take(n_arrays)
    (sems,) = take(1)
    copies = start_copies(list(zip(kv_in, kv_refs)), sems)

    y, c, k = at_ref[2], at_ref[3], at_ref[4]

    def id_of(e, dy, core, x_hi):
        return block_of[(e * 8 + lax.rem(y + dy + N_Y, N_Y) * 2 + core) * 2 + x_hi]

    q_ids = [id_of(s // 2, 0, core, s % 2) for core in (c, 1 - c) for s in range(4)]
    ranks = [
        functools.reduce(
            jnp.add, [(q_ids[u] < q_ids[v]).astype(jnp.int32) for u in range(n_q) if u != v]
        )
        for v in range(n_q)
    ]
    spots = [pl.ds(pl.multiple_of(rank * width_q, width_q), width_q) for rank in ranks]
    if first:
        for v in range(n_q):
            runs = q_parts[v // 4 * 2 : v // 4 * 2 + 2]
            q_sorted[:, spots[v]] = jnp.concatenate([run[v % 4] for run in runs], axis=1)
        acc[...] = jnp.zeros_like(acc)
        top[...] = jnp.full_like(top, LOW)
    else:
        acc[...] = acc_in[...]
        top[...] = top_in[...]

    def place_of(index, ks, e):
        run, inside = index // SUB, index % SUB
        at = (inside // TOK) * (N_Z * TOK) + inside % TOK
        for i, kk in enumerate(ks):
            zh = jnp.where(e == 0, kk, 3 - kk)
            at = at + jnp.where(run == i, zh * TOK, 0)
        return at

    other = 3 - k
    key_ks = [k, k ^ 1, other, other ^ 1]

    def tile(load, offset, width):
        cols = slice(offset, offset + width)
        keys, values, e, near, far = load()
        scores = jnp.dot(keys, q_sorted[:, cols], preferred_element_type=F32)
        key_at = place_of(lax.broadcasted_iota(jnp.int32, (HALF, 1), 0), key_ks, e)
        query = lax.broadcasted_iota(jnp.int32, (1, HALF), 1)
        query_at = place_of(query % width_q, key_ks[:2], e)
        reach = jnp.where(query < width_q, near, far)
        head = jnp.where(key_at <= query_at + reach, scores[:, :HALF], LOW)
        scores = head if width == HALF else jnp.concatenate([head, scores[:, HALF:]], axis=1)
        old = top[:1, cols]
        new = jnp.maximum(old, jnp.max(scores, axis=0, keepdims=True))
        weights = jnp.exp2(scores - new).astype(BF16)
        acc[:, cols] = acc[:, cols] * jnp.exp2(old - new) + jnp.dot(
            values, weights, preferred_element_type=F32
        )
        top[:, cols] = jnp.broadcast_to(new, (8, width))

    def key_block(dy, views, s):
        e = s // 2
        block = id_of(e, dy, c, lax.rem(s, 2))
        count = functools.reduce(jnp.add, [(i >= block).astype(jnp.int32) for i in q_ids])
        same = functools.reduce(jnp.add, [(i == block).astype(jnp.int32) for i in q_ids]) > 0
        odd = lax.rem(count, 2) > 0
        edge = jnp.where(same, 0, 2 * HALF)
        near = jnp.where(odd, -2 * HALF, edge)
        far = jnp.where(odd, edge, 2 * HALF)
        pairs = (count + 1) // 2

        def load():
            runs = [ref[base + s] for ref, base in views]
            keys = jnp.concatenate([r[:SUB] for r in runs], axis=0)
            values = jnp.concatenate([r[SUB:] for r in runs], axis=1)
            values = jnp.concatenate([values, jnp.ones((EXTRA - HD, HALF), BF16)], axis=0)
            return keys, values, e, near, far

        for n in range(1, n_q // 2 + 1):

            @pl.when(pairs == n)
            def _(n=n):
                tile(load, (n_q // 2 - n) * HALF, n * HALF)

    for i, dy in enumerate(steps):
        for copy in copies[2 * i : 2 * i + 2]:
            copy.wait()
        views = [(ref, base) for ref in kv_refs[2 * i : 2 * i + 2] for base in (0, 4)]

        @pl.loop(0, 4)
        def _(s, dy=dy, views=views):
            key_block(dy, views, s)

    if last:
        for v in range(n_q):
            total = acc[HD : HD + 1, spots[v]]
            seen = total > 0
            safe = jnp.where(seen, total, 1.0)
            lse = jnp.where(seen, top[:1, spots[v]] + jnp.log2(safe), LOW)
            high = lse.astype(BF16).astype(F32)
            middle = (lse - high).astype(BF16).astype(F32)
            low = lse - high - middle
            row = lax.broadcasted_iota(jnp.int32, (EXTRA - HD, width_q), 0)
            tail = jnp.where(row == 0, high, jnp.where(row == 1, middle, jnp.where(row == 2, low, 0)))
            cols = slice((v % 4) * width_q, (v % 4 + 1) * width_q)
            outs[v // 4][:HD, cols] = (acc[:HD, spots[v]] / safe).astype(BF16)
            outs[v // 4][HD:, cols] = tail.astype(BF16)


def attend(block_of, at, q_parts, state, steps, arrays, last):
    first = state is None
    q_cols = 4 * HALF
    q_shape, acc_shape, top_shape = (HD, q_cols), (EXTRA, q_cols), (8, q_cols)
    args = list(q_parts if first else state) + list(arrays)
    if last:
        out_shape = [jax.ShapeDtypeStruct((EXTRA, q_cols // 2), BF16)] * 2
        scratch = [pltpu.VMEM(acc_shape, F32), pltpu.VMEM(top_shape, F32)]
    else:
        out_shape = [jax.ShapeDtypeStruct(q_shape, BF16)] if first else []
        out_shape += [
            jax.ShapeDtypeStruct(acc_shape, F32),
            jax.ShapeDtypeStruct(top_shape, F32),
        ]
        scratch = []
    scratch += [pltpu.VMEM(a.shape, a.dtype) for a in arrays]
    scratch.append(pltpu.SemaphoreType.DMA((len(arrays),)))
    pairs = 8 * len(steps)
    outs = pl.pallas_call(
        functools.partial(attend_body, first, last, steps),
        in_specs=[SMEM] * 2 + [VMEM] * (len(args) - len(arrays)) + [HBM] * len(arrays),
        out_specs=[VMEM] * len(out_shape),
        out_shape=out_shape,
        scratch_shapes=scratch,
        compiler_params=pltpu.CompilerParams(vmem_limit_bytes=48 << 20),
        cost_estimate=pl.CostEstimate(
            flops=pairs * HALF * HALF * HD * 4,
            bytes_accessed=6 << 20,
            transcendentals=pairs * HALF * HALF,
        ),
    )(block_of, at, *args)
    if last or first:
        return outs
    return [state[0]] + list(outs)


def merge_body(at_ref, own_ref, other_ref, context_ref):
    parts = [own_ref, other_ref]
    lses = []
    for ref in parts:
        tail = ref[HD:, :].astype(F32)
        lses.append(tail[0:1, :] + tail[1:2, :] + tail[2:3, :])
    top = jnp.maximum(*lses)
    shares = [jnp.exp2(lse - top) for lse in lses]
    mixed = [ref[:HD, :].astype(F32) * share for ref, share in zip(parts, shares)]
    context = ((mixed[0] + mixed[1]) / (shares[0] + shares[1])).T.astype(BF16)
    k = at_ref[4]
    for s in range(4):
        for i in range(2):
            kk = k if i == 0 else k ^ 1
            zh = kk if s < 2 else 3 - kk
            for x_lo in range(2):
                x = (s % 2) * 2 + x_lo
                start = (s * 2 + i) * SUB + x_lo * TOK
                at = pl.ds(pl.multiple_of((x * N_Z + zh) * TOK, TOK), TOK)
                context_ref[at, :] = context[start : start + TOK, :]


def merge(at, own, other):
    return pl.pallas_call(
        merge_body,
        in_specs=[SMEM] + [VMEM] * 2,
        out_specs=VMEM,
        out_shape=jax.ShapeDtypeStruct((own.shape[1], HD), BF16),
        compiler_params=pltpu.CompilerParams(vmem_limit_bytes=12 << 20),
    )(at, own, other)


def output_body(x0, x1, x2, x3, w0, w1, o0, o1, o2, o3):
    rows = jnp.concatenate(
        [
            jnp.concatenate([x[h] for h in range(x.shape[0])], axis=1)
            for x in (x0, x1, x2, x3)
        ],
        axis=0,
    )
    w = jnp.where(pl.program_id(0) < 2, w0[...], w1[...])
    out = jnp.dot(rows, w, preferred_element_type=F32).astype(BF16)
    n = x0.shape[1]
    for i, o in enumerate((o0, o1, o2, o3)):
        o[...] = out[i * n : (i + 1) * n]


def output(parts, ws):
    n = parts[0].shape[1]
    depth, width = ws[0].shape
    tile = 256
    return pl.pallas_call(
        output_body,
        grid=(2 * width // tile,),
        in_specs=[pl.BlockSpec(parts[0].shape, lambda i: (0, 0, 0))] * 4
        + [
            pl.BlockSpec((depth, tile), lambda i: (0, jnp.minimum(i, 1))),
            pl.BlockSpec((depth, tile), lambda i: (0, jnp.maximum(i - 2, 0))),
        ],
        out_specs=[pl.BlockSpec((n, tile), lambda i: (0, i))] * 4,
        out_shape=[jax.ShapeDtypeStruct((n, 2 * width), BF16)] * 4,
        compiler_params=pltpu.CompilerParams(vmem_limit_bytes=20 << 20),
    )(*parts, *ws)


def place_body(at_ref, x0, x1, x2, x3, out_ref):
    y, c = at_ref[2], at_ref[3]
    width = x0.shape[1]
    for d, x in enumerate((x0, x1, x2, x3)):
        quarter = lax.rem(y - d + N_Y, N_Y)
        for i in range(2):
            eighth = 2 * quarter + (c if i == 0 else 1 - c)
            at = pl.multiple_of(eighth * (width // 2), width // 2)
            out_ref[:, pl.ds(at, width // 2)] = x[:, i * width // 2 : (i + 1) * width // 2]


def place(at, parts):
    rows, width = parts[0].shape
    return pl.pallas_call(
        place_body,
        in_specs=[SMEM] + [VMEM] * 4,
        out_specs=VMEM,
        out_shape=jax.ShapeDtypeStruct((rows, 4 * width), BF16),
        compiler_params=pltpu.CompilerParams(vmem_limit_bytes=12 << 20),
    )(at, *parts)


def token_groups():
    groups = []
    for planes in ((0, 2, 5, 7), (1, 3, 4, 6)):
        for y in range(N_Y):
            for c in range(2):
                groups.append([number(x, y, z, c) for x in range(N_X) for z in planes])
    return groups


def shards(tokens, norm_gain, w_qkv, w_out, positions):
    n_uly = lax.axis_size("uly")
    blk, uly = lax.axis_index("blk"), lax.axis_index("uly")
    x, zh = uly // N_Z, uly % N_Z
    z_lo, y, c = blk // 8, (blk // 2) % N_Y, blk % 2
    k = jnp.where(z_lo == 0, zh, 3 - zh)
    at = jnp.stack([x, z_lo, y, c, k]).astype(jnp.int32)
    block_of = positions[::HALF] // HALF

    w = w_qkv[:, 0, :]
    depth = w.shape[0] // 8
    w_part = to_swap(lax.dynamic_slice_in_dim(w, (blk % 8) * depth, depth, 0))
    mirror = to_mirror(tokens)
    normed = norm(tokens, norm_gain)
    own = [normed] + [along_x(normed, d) for d in (-1, 1, 2)]
    w_part = after(w_part, (mirror, own))
    same_z = [list(range(8)), list(range(8, 16))]
    w_other = lax.all_gather(w_part, "blk", axis_index_groups=same_z, axis=0, tiled=True)
    mirror = norm(mirror, norm_gain)
    far = [mirror] + [along_x(mirror, d) for d in (-1, 1, 2)]
    owns = [partial_product(own, w), partial_product(own, w_other)]

    by_piece = positions.reshape(16, N_X, N_Z, TOK)
    even = lax.dynamic_slice(by_piece, (y * 2 + c, 0, k, 0), (1, N_X, 1, TOK))
    odd = lax.dynamic_slice(by_piece, (8 + y * 2 + c, 0, 3 - k, 0), (1, N_X, 1, TOK))
    cos, sin = rope_tables(jnp.concatenate([even.reshape(-1), odd.reshape(-1)]))
    q, kv, other_q, other_kv = project(at, far, [w, w_other], owns, cos, sin)

    swapped, swapped_q = to_swap(other_kv), to_swap(other_q)
    eighth = w_out.shape[2] // N_Y // 2
    w_mine = lax.dynamic_slice_in_dim(w_out[0], (blk % 8) * eighth, eighth, 1)
    w_cols = lax.all_gather(after(w_mine, swapped), "uly", axis=0, tiled=True)

    kv = jnp.concatenate([kv, swapped], axis=0)
    kv_twin = to_twin(kv)
    kv_next, kv_back = along_y(kv, -1), along_y(kv, 1)
    qs = [q, swapped_q, to_other_core(q), to_swap_across(other_q)]
    kv_twin = after(kv_twin, (kv_next, kv_back, qs))

    twin_next, twin_back = along_y(kv_twin, -1), along_y(kv_twin, 1)
    state = attend(block_of, at, qs, None, [0], [kv, kv_twin], False)
    twin_next, twin_back = after((twin_next, twin_back), state[2])
    kv_far = along_y(after(kv_next, (twin_next, twin_back)), -1)
    twin_far = along_y(twin_back, 1)
    state = attend(
        block_of, at, None, state, [1, -1], [kv_next, twin_next, kv_back, twin_back], False
    )
    mine, others = attend(block_of, at, None, state, [2], [kv_far, twin_far], True)
    context = merge(at, mine, to_other_core(others))

    heads = lax.all_to_all(
        context.reshape(n_uly, TOK, HD), BOTH, 0, 0, axis_index_groups=token_groups()
    )
    w_cols = [w_cols, to_other_core(after(w_cols, heads))]
    rows = [heads] + [along_y(heads, -d) for d in (1, 2, 3)]
    made = output(rows, w_cols)
    parts = [made[0]] + [along_y(made[d], d) for d in (1, 2, 3)]
    return place(at, parts)


def solution(mesh):
    placed = (P(("blk", "uly"), None), P(), P(None, "uly", None), P("uly", None, None), P())
    return jax.shard_map(
        shards, mesh=mesh, in_specs=placed, out_specs=P(("blk", "uly"), None), check_vma=False
    )
```
